32 devices in a mesh: clip: 4 (over y, x), feat: 8 (over z, core).
Axes of the slice: x: 2, y: 2, z: 4, core: 2. Of those that a mesh axis runs over, the one named last changes fastest.
Arguments:
- embeds: float32 [4096, 1152], P('clip', 'feat'), may hold values from -6 to 6
- frequencies: float32 [1152, 5120], P('clip', 'feat'), may hold values from -0.5 to 0.5
- phases: float32 [5120], P('feat'), may hold values from -3.140625 to 3.140625
- weights: float32 [5120, 128], P('feat', 'clip'), may hold values from -6 to 6
- labels: int32 [4096, 128], P('clip'), may hold values 0 or 1
Outputs:
- trained: float32 [5120, 128], P('feat', 'clip')
- scores: float32 [4096, 128], P('clip', 'feat')
The draws below stay inside these ranges and needn't reach their ends.
All inputs are finite; a program needn't handle non-finite values. No bound on the sum of `labels` on one device may be relied on, other than what follows from the above.
Results may differ from the reference program's by a relative error of at most 0.0055.
Values may be sent and summed in bfloat16 or wider, within the bound.
No kernel may reach another device: no remote copies, remote signals or barrier semaphores. Data moves between devices by JAX's collectives and lax.ppermute only.
A program may use at most 64 MiB of HBM per device.

```python
import math
import jax
import jax.numpy as jnp
from jax import lax

E = 1152
K = 128
FD = 640
STEPS = 2
NCLIPS = 4096
FEATURES = 5120
N_FEAT = 8


def with_ends(entries, rng, smallest, largest):
    extent = entries.shape
    index_at = [jax.random.randint(jax.random.fold_in(rng, axis), (), 0, extent[axis]) for axis in range(len(extent))]
    entries = entries.at[tuple(index_at)].set(smallest)
    longest = extent.index(max(extent))
    index_at[longest] = (index_at[longest] + 1) % extent[longest]
    return entries.at[tuple(index_at)].set(largest)


def steps_of(rng, shape, split, smallest, largest):
    factor_of = 1.0
    for axis_at, blocks in split:
        draws = jax.random.uniform(jax.random.fold_in(jax.random.fold_in(rng, 6), axis_at), (blocks,), jnp.float32, smallest / len(split), largest / len(split))
        factor_of = factor_of * jnp.repeat(jnp.exp(draws), shape[axis_at] // blocks).reshape((-1,) + (1,) * (len(shape) - 1 - axis_at))
    return factor_of


def bell_draw(rng, dims, deviation, bound, pieces=(), kind=jnp.bfloat16):
    loudness = steps_of(rng, dims, pieces, -0.22, 0.18) if pieces else 1.0
    array = jax.random.normal(rng, dims, jnp.float32) * deviation * loudness
    return jnp.minimum(jnp.maximum(array, -bound), bound).astype(kind)


def setup_inputs(seed: int = 0) -> dict:
    arg_keys = jax.random.split(jax.random.key(seed), 6)
    return {
        "embeds": bell_draw(arg_keys[0], (NCLIPS, E), 1.0, 6.0, ((0, 4), (1, 8)), jnp.float32),
        "frequencies": bell_draw(arg_keys[1], (E, FEATURES), (E // 9) ** -0.5, 0.5, ((0, 4), (1, 8)), jnp.float32),
        "phases": jnp.clip(jax.random.uniform(arg_keys[2], (FEATURES,), jnp.float32, -3.140625, 3.140625), -3.140625, 3.140625),
        "weights": bell_draw(arg_keys[3], (FEATURES, K), 1.0, 6.0, ((0, 8), (1, 4)), jnp.float32),
        "labels": with_ends((jax.random.randint(arg_keys[4], (NCLIPS, K), 0, 2) < 1).astype(jnp.int32), jax.random.fold_in(arg_keys[4], 1), 0, 1),
    }


def features(embeds, frequencies, phases, start):
    columns = lax.dynamic_slice_in_dim(frequencies, start, FD, 1)
    offset = lax.dynamic_slice_in_dim(phases, start, FD, 0)
    angles = jnp.dot(embeds, columns, precision=lax.Precision.HIGHEST, preferred_element_type=jnp.float32)
    feature_scale = math.sqrt(2.0 / FEATURES)
    return (feature_scale * jnp.cos(angles + offset[None, :])).astype(jnp.bfloat16)

def reference(embeds, frequencies, phases, weights, labels):
    starts = jnp.arange(N_FEAT, dtype=jnp.int32) * FD
    targets = labels.astype(jnp.float32)

    def logits_of(beta):
        beta_half = beta.astype(jnp.bfloat16)

        def accumulate(carry, start):
            phi = features(embeds, frequencies, phases, start)
            block = lax.dynamic_slice_in_dim(beta_half, start, FD, 0)
            return (carry + jnp.dot(phi, block, preferred_element_type=jnp.float32), None)
        total, unused = lax.scan(accumulate, jnp.zeros((NCLIPS, K), jnp.float32), starts)
        return total
    beta = weights
    for step in range(STEPS):
        logits = logits_of(beta)
        residual = (jax.nn.sigmoid(logits) - targets).astype(jnp.bfloat16)

        def gradient_block(start):
            phi = features(embeds, frequencies, phases, start)
            return lax.dot_general(phi, residual, (((0,), (0,)), ((), ())), preferred_element_type=jnp.float32)
        gradient = lax.map(gradient_block, starts).reshape(FEATURES, K)
        beta = beta - 0.25 * gradient
    return (beta, logits_of(beta))
```

```python
import math

import jax
import jax.numpy as jnp
from jax import lax
from jax.sharding import PartitionSpec as P

STEPS = 2
EMBED_BOUND = 6.0
FREQ_BOUND = 0.5
CODE_MAX = 32766.0
COS_TURNS = (
    0.9999999890590243,
    -19.739204499454,
    64.93911745989858,
    -85.45013953092679,
    60.16763095123224,
    -25.967599249288032,
    6.528658162158786,
)


def encode(x, bound):
    return jnp.round(x * (CODE_MAX / bound)).astype(jnp.int16)


def split(code):
    wide = code.astype(jnp.int32)
    high = (wide + 128) & ~255
    return high.astype(jnp.bfloat16), (wide - high).astype(jnp.bfloat16)


def folded_ring(n):
    return list(range(0, n, 2)) + list(range(1, n, 2))[::-1]


def core_swap(x):
    n = lax.axis_size("feat")
    return lax.ppermute(x, "feat", [(i, i ^ 1) for i in range(n)])


def line_swap(x, k):
    n = lax.axis_size("feat")
    return lax.ppermute(x, "feat", [(i, i ^ (2 * k)) for i in range(n)])


def clip_swap(x, k):
    n = lax.axis_size("clip")
    return lax.ppermute(x, "clip", [(i, i ^ k) for i in range(n)])


def gather_line(x):
    n = lax.axis_size("feat") // 2
    order = folded_ring(n)
    ring = [(order[i], order[(i + 1) % n]) for i in range(n)]
    perm = [(2 * a + c, 2 * b + c) for a, b in ring for c in range(2)]
    where = [0] * n
    for i, place in enumerate(order):
        where[place] = i
    mine = jnp.asarray(where)[lax.axis_index("feat") // 2]
    found = [(lax.axis_index("feat") // 2, x)]
    for step in range(1, n):
        x = lax.ppermute(x, "feat", perm)
        found.append((jnp.asarray(order)[(mine - step) % n], x))
    return found


def logits_share(partial_value, block):
    lines = lax.axis_size("feat") // 2
    parts = partial_value.reshape(lines, 2, block, -1)
    there = core_swap(parts[:, 1].astype(jnp.bfloat16))
    both = parts[:, 0] + there.astype(jnp.float32)
    half = both.astype(jnp.bfloat16)
    total = both[0]
    for k in range(1, lines):
        total = total + line_swap(half[k], k).astype(jnp.float32)
    return total


def gather_share(share):
    lines = lax.axis_size("feat") // 2
    own = jnp.stack([share] + [line_swap(share, k) for k in range(1, lines)])
    return jnp.stack([own, core_swap(own)], axis=1).reshape(-1, share.shape[-1])


def per_device(embeds, frequencies, phases, weights, labels):
    n_feat, n_clip = lax.axis_size("feat"), lax.axis_size("clip")
    feat, clip = lax.axis_index("feat"), lax.axis_index("clip")
    core = feat % 2
    columns = embeds.shape[1]
    slab, features = frequencies.shape
    total_features = features * n_feat
    outputs = labels.shape[1]
    block = outputs // n_feat

    freq_code = encode(frequencies, FREQ_BOUND)
    embed_code = encode(embeds.T, EMBED_BOUND)
    freq_all = jnp.zeros((n_clip * slab, features), jnp.int16)
    for k in range(n_clip):
        piece = freq_code if k == 0 else clip_swap(freq_code, k)
        freq_all = lax.dynamic_update_slice_in_dim(freq_all, piece, (clip ^ k) * slab, 0)
    embed_all = jnp.zeros((n_feat * columns, embeds.shape[0]), jnp.int16)
    for place, piece in gather_line(embed_code):
        embed_all = lax.dynamic_update_slice_in_dim(embed_all, piece, (2 * place + core) * columns, 0)
        embed_all = lax.dynamic_update_slice_in_dim(
            embed_all, core_swap(piece), (2 * place + 1 - core) * columns, 0
        )

    weights_t = weights.T
    by_clip = jnp.zeros((n_clip, weights_t.shape[0], features), jnp.float32)
    for k in range(n_clip):
        piece = weights_t if k == 0 else clip_swap(weights_t, k)
        by_clip = lax.dynamic_update_slice_in_dim(by_clip, piece[None], clip ^ k, 0)
    by_block = by_clip.reshape(n_feat, block, features)
    beta = jnp.concatenate(
        [lax.dynamic_index_in_dim(by_block, feat ^ b, 0, keepdims=False) for b in range(n_feat)]
    )
    targets = lax.dynamic_slice_in_dim(labels.T, feat * block, block, 0).astype(jnp.float32)

    def dot0(a, b):
        return lax.dot_general(a, b, (((0,), (0,)), ((), ())), preferred_element_type=jnp.float32)

    embed_high, embed_low = split(embed_all)
    freq_high, freq_low = split(freq_all)
    product = dot0(embed_high, freq_high) + (dot0(embed_high, freq_low) + dot0(embed_low, freq_high))
    per_turn = EMBED_BOUND * FREQ_BOUND / (CODE_MAX * CODE_MAX * 2.0 * math.pi)
    turns = product * per_turn + (phases * (0.5 / math.pi))[None, :]
    turns = turns - jnp.round(turns)
    square = turns * turns
    feature_scale = math.sqrt(2.0 / total_features)
    cosine = jnp.full_like(square, COS_TURNS[-1] * feature_scale)
    for coefficient in COS_TURNS[-2::-1]:
        cosine = cosine * square + coefficient * feature_scale
    phi = cosine.astype(jnp.bfloat16)

    def logits_of(beta):
        partial_value = lax.dot_general(
            beta.astype(jnp.bfloat16), phi, (((1,), (1,)), ((), ())), preferred_element_type=jnp.float32
        )
        return logits_share(partial_value, block)

    for step in range(STEPS):
        share = (jax.nn.sigmoid(logits_of(beta)) - targets).astype(jnp.bfloat16)
        residual = gather_share(share)
        grad = jnp.dot(residual, phi, preferred_element_type=jnp.float32)
        sent = grad.astype(jnp.bfloat16)
        total = grad
        for k in range(1, n_clip):
            total = total + clip_swap(sent, k).astype(jnp.float32)
        beta = beta - 0.25 * total
    scores = logits_of(beta).T
    per_clip = n_feat // n_clip
    by_block = beta.reshape(n_feat, block, features)
    trained = jnp.concatenate(
        [
            lax.dynamic_index_in_dim(by_block, feat ^ (clip * per_clip + b), 0, keepdims=False)
            for b in range(per_clip)
        ]
    ).T
    return (trained, scores)


def solution(mesh):
    placed = (P("clip", "feat"), P("clip", "feat"), P("feat"), P("feat", "clip"), P("clip", None))
    return jax.shard_map(
        per_device,
        mesh=mesh,
        in_specs=placed,
        out_specs=(P("feat", "clip"), P("clip", "feat")),
        check_vma=False,
    )
```

```python
import functools
import math

import jax
import jax.numpy as jnp
from jax import lax
from jax.experimental import pallas as pl
from jax.experimental.pallas import tpu as pltpu
from jax.sharding import PartitionSpec as P

STEPS = 2
EMBED_BOUND = 6.0
FREQ_BOUND = 0.5
CODE_MAX = 32766.0
LANES = 128
VMEM_BYTES = 48 * 1024 * 1024
COS_TURNS = (
    0.9999999890590243,
    -19.739204499454,
    64.93911745989858,
    -85.45013953092679,
    60.16763095123224,
    -25.967599249288032,
    6.528658162158786,
)
PER_TURN = EMBED_BOUND * FREQ_BOUND / (CODE_MAX * CODE_MAX * 2.0 * math.pi)


def encode(x, bound):
    return jnp.round(x * (CODE_MAX / bound)).astype(jnp.int16)


def split(code):
    wide = code.astype(jnp.float32)
    high = jnp.round(wide * (1.0 / 256.0)) * 256.0
    return high.astype(jnp.bfloat16), (wide - high).astype(jnp.bfloat16)


def scaled_cos(turns, scale):
    turns = turns - jnp.round(turns)
    square = turns * turns
    value = COS_TURNS[-1] * scale
    for coefficient in COS_TURNS[-2::-1]:
        value = value * square + coefficient * scale
    return value.astype(jnp.bfloat16)


def mix(a, b):
    return jnp.dot(a, b, preferred_element_type=jnp.float32)


def core_swap(x):
    n = lax.axis_size("feat")
    return lax.ppermute(x, "feat", [(i, i ^ 1) for i in range(n)])


def line_swap(x, k):
    n = lax.axis_size("feat")
    return lax.ppermute(x, "feat", [(i, i ^ (2 * k)) for i in range(n)])


def line_move(x, pairs):
    return lax.ppermute(x, "feat", [(2 * a + c, 2 * b + c) for a, b in pairs for c in range(2)])


def clip_swap(x, k):
    n = lax.axis_size("clip")
    return lax.ppermute(x, "clip", [(i, i ^ k) for i in range(n)])


def farthest_first(n):
    return range(n - 1, 0, -1)


def gather_four(x, line):
    second = line_swap(x, 2)
    first = line_swap(x, 1)
    middle = line_move(x, [(1, 2), (2, 1)])
    passed = line_move(second, [(1, 0), (2, 3)])
    third = jnp.where((line == 1) | (line == 2), middle, passed)
    return [x, first, second, third]


def early_kernel(at_ref, *refs, slabs, columns):
    embeds, freqs = refs[: 2 * slabs - 2], refs[2 * slabs - 2 : 3 * slabs - 2]
    sum_ref, high_ref, low_ref, freq_ref, f_high, f_low, e_high, e_low = refs[3 * slabs - 2 :]
    depth = e_high.shape[0]
    used = len(embeds) * columns
    for m, ref in enumerate(freqs):
        for h in range(2):
            row = pl.multiple_of(at_ref[2 * m + h], 16)
            freq_ref[pl.ds(row, columns), :] = ref[h * columns : (h + 1) * columns, :].astype(jnp.float32)
    if depth > used:
        freq_ref[used:depth, :] = jnp.zeros((depth - used, freq_ref.shape[1]), jnp.float32)
        e_high[used:depth, :] = jnp.zeros((depth - used, e_high.shape[1]), jnp.bfloat16)
        e_low[used:depth, :] = jnp.zeros((depth - used, e_low.shape[1]), jnp.bfloat16)

    def halves(x):
        high = jnp.round(x * (1.0 / 256.0)) * 256.0
        return high.astype(jnp.bfloat16), (x - high).astype(jnp.bfloat16)

    for start in range(0, depth, LANES):
        f_high[:, start : start + LANES], f_low[:, start : start + LANES] = halves(
            freq_ref[start : start + LANES, :].T
        )
    high_ref[...], low_ref[...] = halves(freq_ref[depth:, :].T)
    for i, ref in enumerate(embeds):
        rows = slice(i * columns, (i + 1) * columns)
        e_high[rows, :], e_low[rows, :] = halves(ref[...].astype(jnp.float32))
    tile = 256 if sum_ref.shape[1] % 256 == 0 else sum_ref.shape[1]
    for start in range(0, sum_ref.shape[1], tile):
        at = slice(start, start + tile)
        sum_ref[:, at] = mix(f_high[...], e_high[:, at]) + (
            mix(f_high[...], e_low[:, at]) + mix(f_low[...], e_high[:, at])
        )


def late_kernel(sum_ref, own_ref, other_ref, high_ref, low_ref, phase_ref, phi_ref, e_high, e_low, *, columns, scale):
    for i, ref in enumerate((own_ref, other_ref)):
        rows = slice(i * columns, (i + 1) * columns)
        e_high[rows, :], e_low[rows, :] = split(ref[...])
    tile = 256 if sum_ref.shape[1] % 256 == 0 else sum_ref.shape[1]
    for start in range(0, sum_ref.shape[1], tile):
        at = slice(start, start + tile)
        total = sum_ref[:, at] + (
            mix(high_ref[...], e_high[:, at])
            + (mix(high_ref[...], e_low[:, at]) + mix(low_ref[...], e_high[:, at]))
        )
        phi_ref[:, at] = scaled_cos(total * PER_TURN + phase_ref[...], scale)


def phi_by_kernels(embed_code, freq_code, phase_turns, scale, line, core, clip):
    slabs = lax.axis_size("clip")
    columns, clips = embed_code.shape
    features = freq_code.shape[1]
    own = gather_four(embed_code, line)
    freqs = [freq_code] + [clip_swap(freq_code, k) for k in range(1, slabs)]
    other = [core_swap(x) for x in own]
    used = 2 * (slabs - 1) * columns
    depth = -(-used // LANES) * LANES
    places = []
    for m in range(slabs):
        k = m ^ line ^ clip
        base = k * 2 * columns + jnp.where(k == slabs - 1, depth - used, 0)
        places += [base + core * columns, base + (1 - core) * columns]
    early = [x for k in range(slabs - 1) for x in (own[k], other[k])]
    vmem = pl.BlockSpec(memory_space=pltpu.VMEM)
    summed, high, low = pl.pallas_call(
        functools.partial(early_kernel, slabs=slabs, columns=columns),
        out_shape=(
            jax.ShapeDtypeStruct((features, clips), jnp.float32),
            jax.ShapeDtypeStruct((features, 2 * columns), jnp.bfloat16),
            jax.ShapeDtypeStruct((features, 2 * columns), jnp.bfloat16),
        ),
        in_specs=[pl.BlockSpec(memory_space=pltpu.SMEM)] + [vmem] * (len(early) + slabs),
        out_specs=(vmem, vmem, vmem),
        scratch_shapes=[
            pltpu.VMEM((depth + 2 * columns, features), jnp.float32),
            pltpu.VMEM((features, depth), jnp.bfloat16),
            pltpu.VMEM((features, depth), jnp.bfloat16),
            pltpu.VMEM((depth, clips), jnp.bfloat16),
            pltpu.VMEM((depth, clips), jnp.bfloat16),
        ],
        compiler_params=pltpu.CompilerParams(vmem_limit_bytes=VMEM_BYTES),
        cost_estimate=pl.CostEstimate(
            flops=6 * features * depth * clips, bytes_accessed=8 * features * clips, transcendentals=0
        ),
        name="early_angles",
    )(jnp.stack(places).astype(jnp.int32), *early, *freqs)
    return pl.pallas_call(
        functools.partial(late_kernel, columns=columns, scale=scale),
        out_shape=jax.ShapeDtypeStruct((features, clips), jnp.bfloat16),
        in_specs=[vmem] * 6,
        out_specs=vmem,
        scratch_shapes=[pltpu.VMEM((2 * columns, clips), jnp.bfloat16)] * 2,
        compiler_params=pltpu.CompilerParams(vmem_limit_bytes=VMEM_BYTES),
        cost_estimate=pl.CostEstimate(
            flops=6 * features * 2 * columns * clips, bytes_accessed=6 * features * clips, transcendentals=0
        ),
        name="late_angles",
    )(summed, own[-1], other[-1], high, low, phase_turns[:, None])


def phi_by_ring(embed_code, freq_code, phase_turns, scale, line, core, clip):
    places, n_clip = lax.axis_size("feat") // 2, lax.axis_size("clip")
    columns, clips = embed_code.shape
    slab, features = freq_code.shape
    freq_all = jnp.zeros((n_clip * slab, features), jnp.int16)
    for k in range(n_clip):
        piece = freq_code if k == 0 else clip_swap(freq_code, k)
        freq_all = lax.dynamic_update_slice_in_dim(freq_all, piece, (clip ^ k) * slab, 0)
    embed_all = jnp.zeros((2 * places * columns, clips), jnp.int16)
    piece = embed_code
    ring = [(i, (i + 1) % places) for i in range(places)]
    for step in range(places):
        if step:
            piece = line_move(piece, ring)
        base = 2 * ((line - step) % places)
        embed_all = lax.dynamic_update_slice_in_dim(embed_all, piece, (base + core) * columns, 0)
        embed_all = lax.dynamic_update_slice_in_dim(
            embed_all, core_swap(piece), (base + 1 - core) * columns, 0
        )

    def dot0(a, b):
        return lax.dot_general(a, b, (((0,), (0,)), ((), ())), preferred_element_type=jnp.float32)

    embed_high, embed_low = split(embed_all)
    freq_high, freq_low = split(freq_all)
    total = dot0(freq_high, embed_high) + (dot0(freq_high, embed_low) + dot0(freq_low, embed_high))
    return scaled_cos(total * PER_TURN + phase_turns[:, None], scale)


def per_device(embeds, frequencies, phases, weights, labels):
    n_feat, n_clip = lax.axis_size("feat"), lax.axis_size("clip")
    feat, clip = lax.axis_index("feat"), lax.axis_index("clip")
    places, line, core = n_feat // 2, feat // 2, feat % 2
    columns = embeds.shape[1]
    features = frequencies.shape[1]
    outputs = labels.shape[1]
    block = outputs // n_feat
    scale = math.sqrt(2.0 / (features * n_feat))

    freq_code = encode(frequencies, FREQ_BOUND)
    embed_code = encode(embeds.T, EMBED_BOUND)
    phase_turns = phases * (0.5 / math.pi)
    by_kernels = places == 4 and n_clip == 4 and columns % 16 == 0 and frequencies.shape[0] == 2 * columns
    phi_of = phi_by_kernels if by_kernels else phi_by_ring
    phi = phi_of(embed_code, freq_code, phase_turns, scale, line, core, clip)
    phi_other = core_swap(phi)

    weights_t = weights.T
    by_clip = jnp.zeros((n_clip, weights_t.shape[0], features), jnp.float32)
    for k in range(n_clip):
        piece = weights_t if k == 0 else clip_swap(weights_t, k)
        by_clip = lax.dynamic_update_slice_in_dim(by_clip, piece[None], clip ^ k, 0)
    by_block = by_clip.reshape(n_feat, block, features)

    def blocks_of(side):
        return jnp.concatenate(
            [
                lax.dynamic_index_in_dim(by_block, 2 * (line ^ k) + side, 0, keepdims=False)
                for k in range(places)
            ]
        )

    beta = blocks_of(core)
    beta_other = core_swap(blocks_of(1 - core))
    targets = lax.dynamic_slice_in_dim(labels.T, feat * block, block, 0).astype(jnp.float32)

    def logits_of(beta, beta_other):
        value = mix(beta.astype(jnp.bfloat16), phi) + mix(beta_other.astype(jnp.bfloat16), phi_other)
        parts = value.reshape(places, block, -1)
        half = parts.astype(jnp.bfloat16)
        total = parts[0]
        for k in farthest_first(places):
            total = total + line_swap(half[k], k).astype(jnp.float32)
        return total

    def gradient_of(residual, phi):
        return lax.dot_general(residual, phi, (((1,), (1,)), ((), ())), preferred_element_type=jnp.float32)

    for step in range(STEPS):
        share = (jax.nn.sigmoid(logits_of(beta, beta_other)) - targets).astype(jnp.bfloat16)
        found = {k: line_swap(share, k) for k in farthest_first(places)}
        residual = jnp.concatenate([share] + [found[k] for k in range(1, places)])
        grad = jnp.concatenate([gradient_of(residual, phi), gradient_of(residual, phi_other)], axis=1)
        sent = grad.astype(jnp.bfloat16)
        for k in farthest_first(n_clip):
            grad = grad + clip_swap(sent, k).astype(jnp.float32)
        beta = beta - 0.25 * grad[:, :features]
        beta_other = beta_other - 0.25 * grad[:, features:]
    scores = logits_of(beta, beta_other).T
    ours = beta.reshape(places, block, features)
    theirs = core_swap(beta_other).reshape(places, block, features)
    rows = []
    for b in range(places // n_clip):
        k = line ^ (clip * (places // n_clip) + b)
        mine = lax.dynamic_index_in_dim(ours, k, 0, keepdims=False)
        their = lax.dynamic_index_in_dim(theirs, k, 0, keepdims=False)
        rows += [jnp.where(core == 0, mine, their), jnp.where(core == 0, their, mine)]
    trained = jnp.concatenate(rows).T
    return (trained, scores)


def solution(mesh):
    placed = (P("clip", "feat"), P("clip", "feat"), P("feat"), P("feat", "clip"), P("clip", None))
    return jax.shard_map(
        per_device,
        mesh=mesh,
        in_specs=placed,
        out_specs=(P("feat", "clip"), P("clip", "feat")),
        check_vma=False,
    )
```

```python
import functools
import math

import jax
import jax.numpy as jnp
from jax import lax
from jax.experimental import pallas as pl
from jax.experimental.pallas import tpu as pltpu
from jax.sharding import PartitionSpec as P

STEPS = 2
EMBED_BOUND = 6.0
FREQ_BOUND = 0.5
CODE_MAX = 32766.0
LANES = 128
VMEM_BYTES = 13 * 1024 * 1024
COS_TURNS = (
    0.9999999890590243,
    -19.739204499454,
    64.93911745989858,
    -85.45013953092679,
    60.16763095123224,
    -25.967599249288032,
    6.528658162158786,
)
PER_TURN = EMBED_BOUND * FREQ_BOUND / (CODE_MAX * CODE_MAX * 2.0 * math.pi)


def encode(x, bound):
    return jnp.round(x * (CODE_MAX / bound)).astype(jnp.int16)


def split(code):
    wide = code.astype(jnp.float32)
    high = jnp.round(wide * (1.0 / 256.0)) * 256.0
    return high.astype(jnp.bfloat16), (wide - high).astype(jnp.bfloat16)


def scaled_cos(turns, scale):
    turns = turns - jnp.round(turns)
    square = turns * turns
    value = COS_TURNS[-1] * scale
    for coefficient in COS_TURNS[-2::-1]:
        value = value * square + coefficient * scale
    return value.astype(jnp.bfloat16)


def mix(a, b):
    return jnp.dot(a, b, preferred_element_type=jnp.float32)


def core_swap(x):
    n = lax.axis_size("feat")
    return lax.ppermute(x, "feat", [(i, i ^ 1) for i in range(n)])


def line_swap(x, k):
    n = lax.axis_size("feat")
    return lax.ppermute(x, "feat", [(i, i ^ (2 * k)) for i in range(n)])


def line_move(x, pairs):
    return lax.ppermute(x, "feat", [(2 * a + c, 2 * b + c) for a, b in pairs for c in range(2)])


def clip_swap(x, k):
    n = lax.axis_size("clip")
    return lax.ppermute(x, "clip", [(i, i ^ k) for i in range(n)])


def farthest_first(n):
    return range(n - 1, 0, -1)


def halves(x):
    high = jnp.round(x * (1.0 / 256.0)) * 256.0
    return high.astype(jnp.bfloat16), (x - high).astype(jnp.bfloat16)


def copied(sources, places, sem):
    copies = [pltpu.make_async_copy(a, b, sem.at[i]) for i, (a, b) in enumerate(zip(sources, places))]
    for copy in copies:
        copy.start()
    return copies


def tiles_of(ref):
    tile = 256 if ref.shape[1] % 256 == 0 else ref.shape[1]
    return [slice(start, start + tile) for start in range(0, ref.shape[1], tile)]


def early_kernel(
    at_ref, *refs, n_embeds, n_freqs, columns
):
    embeds, freqs = refs[:n_embeds], refs[n_embeds : n_embeds + n_freqs]
    (
        sum_ref, high_ref, low_ref, freq_code, embed_code, f_high, f_low, e_high, e_low, sem_f, sem_e,
    ) = refs[n_embeds + n_freqs :]
    depth = e_high.shape[0]
    used = n_embeds * columns
    rows = [pl.ds(pl.multiple_of(at_ref[i], 16), columns) for i in range(2 * n_freqs)]
    pieces = [ref.at[h * columns : (h + 1) * columns, :] for ref in freqs for h in range(2)]
    of_freqs = copied(pieces, [freq_code.at[r, :] for r in rows], sem_f)
    of_embeds = copied(embeds, [embed_code.at[i * columns : (i + 1) * columns, :] for i in range(n_embeds)], sem_e)
    if depth > used:
        freq_code[used:depth, :] = jnp.zeros((depth - used, freq_code.shape[1]), jnp.int16)
        embed_code[used:depth, :] = jnp.zeros((depth - used, embed_code.shape[1]), jnp.int16)
    for copy in of_embeds:
        copy.wait()
    e_high[...], e_low[...] = halves(embed_code[...].astype(jnp.float32))
    for copy in of_freqs:
        copy.wait()
    for start in range(0, depth, LANES):
        f_high[:, start : start + LANES], f_low[:, start : start + LANES] = halves(
            freq_code[start : start + LANES, :].astype(jnp.float32).T
        )
    high_ref[...], low_ref[...] = halves(freq_code[depth:, :].astype(jnp.float32).T)
    for at in tiles_of(sum_ref):
        sum_ref[:, at] = mix(f_high[...], e_high[:, at]) + (
            mix(f_high[...], e_low[:, at]) + mix(f_low[...], e_high[:, at])
        )


def late_kernel(
    pick_ref, sum_ref, own_a, own_b, other_a, other_b, high_ref, low_ref, phase_ref,
    phi_ref, embed_code, e_high, e_low, sem_e, *, columns, scale,
):
    @pl.when(pick_ref[0] == 1)
    def _():
        copied((own_a, other_a), (embed_code.at[:columns], embed_code.at[columns:]), sem_e)

    @pl.when(pick_ref[0] != 1)
    def _():
        copied((own_b, other_b), (embed_code.at[:columns], embed_code.at[columns:]), sem_e)

    for i in range(2):
        half = embed_code.at[i * columns : (i + 1) * columns]
        pltpu.make_async_copy(own_a, half, sem_e.at[i]).wait()
    e_high[...], e_low[...] = halves(embed_code[...].astype(jnp.float32))
    for at in tiles_of(sum_ref):
        total = sum_ref[:, at] + (
            mix(high_ref[...], e_high[:, at])
            + (mix(high_ref[...], e_low[:, at]) + mix(low_ref[...], e_high[:, at]))
        )
        phi_ref[:, at] = scaled_cos(total * PER_TURN + phase_ref[...], scale)


def phi_by_kernels(embed_code, frequencies, scale, line, core, clip, weights_in):
    slabs = 4
    columns, clips = embed_code.shape
    features = frequencies.shape[1]
    tie = lax.optimization_barrier
    freq = encode(frequencies, FREQ_BOUND)
    second = line_swap(embed_code, 2)
    first = line_swap(embed_code, 1)
    freq_xy, freq_x, freq_y = [clip_swap(freq, k) for k in (3, 1, 2)]
    second, first, freq_xy, freq_x, freq_y, embed_again = tie((second, first, freq_xy, freq_x, freq_y, embed_code))
    passed = line_move(second, [(1, 0), (2, 3)])
    middle = line_move(embed_again, [(1, 2), (2, 1)])
    own = [embed_again, first, second]
    other = tie(tuple(core_swap(x) for x in own) + (weights_in[2],))
    early = [y for pair in zip(own, other) for y in pair]
    beta, targets, column = weights_in[1](weights_in[0](other[-1]))
    freqs = [freq, freq_x, freq_y, freq_xy]
    used = len(early) * columns
    depth = -(-used // LANES) * LANES
    at = []
    for m in range(slabs):
        k = m ^ line ^ clip
        base = k * 2 * columns + jnp.where(k == slabs - 1, depth - used, 0)
        at += [base + core * columns, base + (1 - core) * columns]
    vmem = pl.BlockSpec(memory_space=pltpu.VMEM)
    smem = pl.BlockSpec(memory_space=pltpu.SMEM)
    anywhere = pl.BlockSpec(memory_space=pl.ANY)
    params = pltpu.CompilerParams(vmem_limit_bytes=VMEM_BYTES)
    summed, high, low = pl.pallas_call(
        functools.partial(early_kernel, n_embeds=len(early), n_freqs=len(freqs), columns=columns),
        out_shape=(
            jax.ShapeDtypeStruct((features, clips), jnp.float32),
            jax.ShapeDtypeStruct((features, 2 * columns), jnp.bfloat16),
            jax.ShapeDtypeStruct((features, 2 * columns), jnp.bfloat16),
        ),
        in_specs=[smem] + [anywhere] * (len(early) + len(freqs)),
        out_specs=(vmem, vmem, vmem),
        scratch_shapes=[
            pltpu.VMEM((depth + 2 * columns, features), jnp.int16),
            pltpu.VMEM((depth, clips), jnp.int16),
            pltpu.VMEM((features, depth), jnp.bfloat16),
            pltpu.VMEM((features, depth), jnp.bfloat16),
            pltpu.VMEM((depth, clips), jnp.bfloat16),
            pltpu.VMEM((depth, clips), jnp.bfloat16),
            pltpu.SemaphoreType.DMA((2 * len(freqs),)),
            pltpu.SemaphoreType.DMA((len(early),)),
        ],
        compiler_params=params,
        cost_estimate=pl.CostEstimate(
            flops=6 * features * depth * clips, bytes_accessed=8 * features * clips, transcendentals=0
        ),
        name="early_angles",
    )(jnp.stack(at).astype(jnp.int32), *early, *freqs)
    pick = jnp.where((line == 1) | (line == 2), 1, 0).astype(jnp.int32)[None]
    phi = pl.pallas_call(
        functools.partial(late_kernel, columns=columns, scale=scale),
        out_shape=jax.ShapeDtypeStruct((features, clips), jnp.bfloat16),
        in_specs=[smem, vmem] + [anywhere] * 4 + [vmem] * 3,
        out_specs=vmem,
        scratch_shapes=[
            pltpu.VMEM((2 * columns, clips), jnp.int16),
            pltpu.VMEM((2 * columns, clips), jnp.bfloat16),
            pltpu.VMEM((2 * columns, clips), jnp.bfloat16),
            pltpu.SemaphoreType.DMA((2,)),
        ],
        compiler_params=params,
        cost_estimate=pl.CostEstimate(
            flops=6 * features * 2 * columns * clips, bytes_accessed=6 * features * clips, transcendentals=0
        ),
        name="late_angles",
    )(pick, summed, middle, passed, core_swap(middle), core_swap(passed), high, low, column)
    return phi, beta, targets


def phi_by_ring(embed_code, frequencies, scale, line, core, clip, weights_in):
    freq_code = encode(frequencies, FREQ_BOUND)
    places, n_clip = lax.axis_size("feat") // 2, lax.axis_size("clip")
    columns, clips = embed_code.shape
    slab, features = freq_code.shape
    freq_all = jnp.zeros((n_clip * slab, features), jnp.int16)
    for k in range(n_clip):
        piece = freq_code if k == 0 else clip_swap(freq_code, k)
        freq_all = lax.dynamic_update_slice_in_dim(freq_all, piece, (clip ^ k) * slab, 0)
    embed_all = jnp.zeros((2 * places * columns, clips), jnp.int16)
    piece = embed_code
    ring = [(i, (i + 1) % places) for i in range(places)]
    for step in range(places):
        if step:
            piece = line_move(piece, ring)
        base = 2 * ((line - step) % places)
        embed_all = lax.dynamic_update_slice_in_dim(embed_all, piece, (base + core) * columns, 0)
        embed_all = lax.dynamic_update_slice_in_dim(
            embed_all, core_swap(piece), (base + 1 - core) * columns, 0
        )

    def dot0(a, b):
        return lax.dot_general(a, b, (((0,), (0,)), ((), ())), preferred_element_type=jnp.float32)

    embed_high, embed_low = split(embed_all)
    freq_high, freq_low = split(freq_all)
    total = dot0(freq_high, embed_high) + (dot0(freq_high, embed_low) + dot0(freq_low, embed_high))
    beta, targets, column = weights_in[1](weights_in[0](weights_in[2]))
    return scaled_cos(total * PER_TURN + column, scale), beta, targets


def per_device(embeds, frequencies, phases, weights, labels):
    n_feat, n_clip = lax.axis_size("feat"), lax.axis_size("clip")
    feat, clip = lax.axis_index("feat"), lax.axis_index("clip")
    places, line, core = n_feat // 2, feat // 2, feat % 2
    columns = embeds.shape[1]
    features = frequencies.shape[1]
    outputs = labels.shape[1]
    block = outputs // n_feat
    scale = math.sqrt(2.0 / (features * n_feat))

    embed_code = encode(embeds.T, EMBED_BOUND)
    phase_turns = phases * (0.5 / math.pi)
    by_kernels = places == 4 and n_clip == 4 and columns % 16 == 0 and frequencies.shape[0] == 2 * columns
    per_clip = places // n_clip

    def weights_in(weights):
        piece = weights.T
        return [piece] + [clip_swap(piece, k) for k in range(1, n_clip)]

    def weights_of(pieces):
        stacked = jnp.concatenate(pieces).reshape(n_clip * per_clip, 2, block, features)

        def ordered(side):
            rows = lax.dynamic_index_in_dim(stacked, side, 1, keepdims=False)
            found = []
            for k in range(places):
                place = line ^ k
                at = ((place // per_clip) ^ clip) * per_clip + place % per_clip
                found.append(lax.dynamic_index_in_dim(rows, at, 0, keepdims=False))
            return jnp.concatenate(found)

        beta_own, beta_sent = ordered(core), ordered(1 - core)
        targets = lax.dynamic_slice_in_dim(labels.T, feat * block, block, 0).astype(jnp.float32)
        return (beta_own, beta_sent, core_swap(beta_sent)), targets, phase_turns[:, None]

    def share_of(parts):
        parts = parts.reshape(places, block, -1)
        half = parts.astype(jnp.bfloat16)
        total = parts[0]
        found = [line_swap(half[k], k) for k in farthest_first(places)]
        return total, found

    def add_up(total, found):
        for x in found:
            total = total + x.astype(jnp.float32)
        return total

    def gradient_of(residual, phi):
        return lax.dot_general(residual, phi, (((1,), (1,)), ((), ())), preferred_element_type=jnp.float32)

    phi_of = phi_by_kernels if by_kernels else phi_by_ring
    phi, beta, targets = phi_of(
        embed_code, frequencies, scale, line, core, clip, (weights_in, weights_of, weights)
    )
    beta_own, beta_sent, beta_other = beta
    there = core_swap(mix(beta_sent.astype(jnp.bfloat16), phi).astype(jnp.bfloat16))
    parts = mix(beta_own.astype(jnp.bfloat16), phi) + there.astype(jnp.float32)
    phi_other = core_swap(phi)
    for step in range(STEPS):
        share = (jax.nn.sigmoid(add_up(*share_of(parts))) - targets).astype(jnp.bfloat16)
        found = {k: line_swap(share, k) for k in farthest_first(places)}
        residual = jnp.concatenate([share] + [found[k] for k in range(1, places)])
        grad = jnp.concatenate([gradient_of(residual, phi), gradient_of(residual, phi_other)], axis=1)
        sent = grad.astype(jnp.bfloat16)
        for k in farthest_first(n_clip):
            grad = grad + clip_swap(sent, k).astype(jnp.float32)
        beta_own = beta_own - 0.25 * grad[:, :features]
        beta_other = beta_other - 0.25 * grad[:, features:]
        parts = mix(beta_own.astype(jnp.bfloat16), phi) + mix(beta_other.astype(jnp.bfloat16), phi_other)
    total, found = share_of(parts)
    ours = beta_own.reshape(places, block, features)
    theirs = core_swap(beta_other).reshape(places, block, features)
    rows = []
    for b in range(per_clip):
        k = line ^ (clip * per_clip + b)
        mine = lax.dynamic_index_in_dim(ours, k, 0, keepdims=False)
        their = lax.dynamic_index_in_dim(theirs, k, 0, keepdims=False)
        rows += [jnp.where(core == 0, mine, their), jnp.where(core == 0, their, mine)]
    trained, total = lax.optimization_barrier((jnp.concatenate(rows).T, total))
    return (trained, add_up(total, found).T)


def solution(mesh):
    placed = (P("clip", "feat"), P("clip", "feat"), P("feat"), P("feat", "clip"), P("clip", None))
    return jax.shard_map(
        per_device,
        mesh=mesh,
        in_specs=placed,
        out_specs=(P("feat", "clip"), P("clip", "feat")),
        check_vma=False,
    )
```

```python
import functools
import math

import jax
import jax.numpy as jnp
from jax import lax
from jax.experimental import pallas as pl
from jax.experimental.pallas import tpu as pltpu
from jax.sharding import PartitionSpec as P

STEPS = 2
EMBED_BOUND = 6.0
FREQ_BOUND = 0.5
CODE_MAX = 32766.0
LANES = 128
VMEM_BYTES = 16 * 1024 * 1024
EARLY_VMEM_BYTES = 56 * 1024 * 1024
WEIGHT_BOUND = 6.0
COS_TURNS = (
    0.9999999890590243,
    -19.739204499454,
    64.93911745989858,
    -85.45013953092679,
    60.16763095123224,
    -25.967599249288032,
    6.528658162158786,
)
PER_TURN = EMBED_BOUND * FREQ_BOUND / (CODE_MAX * CODE_MAX * 2.0 * math.pi)


def encode(x, bound):
    return jnp.round(x * (CODE_MAX / bound)).astype(jnp.int16)


def split(code):
    wide = code.astype(jnp.float32)
    high = jnp.round(wide * (1.0 / 256.0)) * 256.0
    return high.astype(jnp.bfloat16), (wide - high).astype(jnp.bfloat16)


def scaled_cos(turns, scale):
    turns = turns - jnp.round(turns)
    square = turns * turns
    value = COS_TURNS[-1] * scale
    for coefficient in COS_TURNS[-2::-1]:
        value = value * square + coefficient * scale
    return value.astype(jnp.bfloat16)


def mix(a, b):
    return jnp.dot(a, b, preferred_element_type=jnp.float32)


def core_swap(x):
    n = lax.axis_size("feat")
    return lax.ppermute(x, "feat", [(i, i ^ 1) for i in range(n)])


def line_swap(x, k):
    n = lax.axis_size("feat")
    return lax.ppermute(x, "feat", [(i, i ^ (2 * k)) for i in range(n)])


def line_move(x, pairs):
    return lax.ppermute(x, "feat", [(2 * a + c, 2 * b + c) for a, b in pairs for c in range(2)])


def clip_swap(x, k):
    n = lax.axis_size("clip")
    return lax.ppermute(x, "clip", [(i, i ^ k) for i in range(n)])


def farthest_first(n):
    return range(n - 1, 0, -1)


def halves(x):
    high = jnp.round(x * (1.0 / 256.0)) * 256.0
    return high.astype(jnp.bfloat16), (x - high).astype(jnp.bfloat16)


def copied(sources, places, sem):
    copies = [pltpu.make_async_copy(a, b, sem.at[i]) for i, (a, b) in enumerate(zip(sources, places))]
    for copy in copies:
        copy.start()
    return copies


def tiles_of(ref):
    tile = 256 if ref.shape[1] % 256 == 0 else ref.shape[1]
    return [slice(start, start + tile) for start in range(0, ref.shape[1], tile)]


def early_kernel(
    at_ref, *refs, n_embeds, n_freqs, columns
):
    embeds, freqs = refs[:n_embeds], refs[n_embeds : n_embeds + n_freqs]
    (
        sum_ref, high_ref, low_ref, freq_code, embed_code, f_high, f_low, e_high, e_low, sem_f, sem_e,
    ) = refs[n_embeds + n_freqs :]
    depth = e_high.shape[0]
    used = n_embeds * columns
    line, clip, core = at_ref[0], at_ref[1], at_ref[2]

    def on_ring(place):
        return jnp.where(place == 0, 0, jnp.where(place == 1, 3, place - 1))

    rows = []
    for m in range(n_freqs // 2):
        step = (on_ring(line) - on_ring(clip ^ m)) & 3
        base = step * 2 * columns + jnp.where(step == 3, depth - used, 0)
        rows += [pl.ds(pl.multiple_of(base + h * columns, 16), columns) for h in (core, 1 - core)]
    pieces = [ref.at[:columns, :] for ref in freqs]
    of_freqs = copied(pieces, [freq_code.at[r, :] for r in rows], sem_f)
    of_embeds = copied(embeds, [embed_code.at[i * columns : (i + 1) * columns, :] for i in range(n_embeds)], sem_e)
    if depth > used:
        freq_code[used:depth, :] = jnp.zeros((depth - used, freq_code.shape[1]), jnp.int16)
        embed_code[used:depth, :] = jnp.zeros((depth - used, embed_code.shape[1]), jnp.int16)
    for copy in of_embeds:
        copy.wait()
    e_high[...], e_low[...] = halves(embed_code[...].astype(jnp.float32))
    for copy in of_freqs:
        copy.wait()
    for start in range(0, depth, LANES):
        f_high[:, start : start + LANES], f_low[:, start : start + LANES] = halves(
            freq_code[start : start + LANES, :].T.astype(jnp.float32)
        )
    high_ref[...], low_ref[...] = halves(freq_code[depth:, :].T.astype(jnp.float32))
    for at in tiles_of(sum_ref):
        sum_ref[:, at] = mix(f_high[...], e_high[:, at]) + (
            mix(f_high[...], e_low[:, at]) + mix(f_low[...], e_high[:, at])
        )


def late_kernel(
    sum_ref, own_ref, other_ref, high_ref, low_ref, phase_ref,
    phi_ref, sums, embed_code, e_high, e_low, sem_s, sem_e, *, columns, scale,
):
    of_embeds = copied((own_ref, other_ref), (embed_code.at[:columns], embed_code.at[columns:]), sem_e)
    of_sums = copied((sum_ref,), (sums,), sem_s)
    for copy in of_embeds:
        copy.wait()
    e_high[...], e_low[...] = halves(embed_code[...].astype(jnp.float32))
    for copy in of_sums:
        copy.wait()
    for at in tiles_of(sums):
        total = sums[:, at] + (
            mix(high_ref[...], e_high[:, at])
            + (mix(high_ref[...], e_low[:, at]) + mix(low_ref[...], e_high[:, at]))
        )
        phi_ref[:, at] = scaled_cos(total * PER_TURN + phase_ref[...], scale)


def phi_by_kernels(embed_code, freq_code, column, scale, line, core, clip, prepare):
    slabs = 4
    columns, clips = embed_code.shape
    features = freq_code[0].shape[1]
    tie = lax.optimization_barrier
    x_low, y_high = clip_swap(freq_code[0], 1), clip_swap(freq_code[1], 2)
    x_high, y_low = clip_swap(freq_code[1], 1), clip_swap(freq_code[0], 2)
    freqs = [*freq_code, x_low, x_high, y_low, y_high, clip_swap(x_low, 2), clip_swap(y_high, 1)]
    ring = [(0, 2), (2, 3), (3, 1), (1, 0)]
    own = [embed_code]
    for _ in range(slabs - 1):
        own.append(line_move(own[-1], ring))
    other = [core_swap(own[0]), core_swap(own[1])]
    *freqs, turn = tie((*freqs, own[2]))
    other.append(core_swap(turn))
    rest = prepare(freqs)
    early = [x for pair in zip(own[:3], other) for x in pair]
    used = len(early) * columns
    depth = -(-used // LANES) * LANES
    vmem = pl.BlockSpec(memory_space=pltpu.VMEM)
    smem = pl.BlockSpec(memory_space=pltpu.SMEM)
    anywhere = pl.BlockSpec(memory_space=pl.ANY)
    summed, high, low = pl.pallas_call(
        functools.partial(early_kernel, n_embeds=len(early), n_freqs=len(freqs), columns=columns),
        out_shape=(
            jax.ShapeDtypeStruct((features, clips), jnp.float32),
            jax.ShapeDtypeStruct((features, 2 * columns), jnp.bfloat16),
            jax.ShapeDtypeStruct((features, 2 * columns), jnp.bfloat16),
        ),
        in_specs=[smem] + [anywhere] * (len(early) + len(freqs)),
        out_specs=(vmem, vmem, vmem),
        scratch_shapes=[
            pltpu.VMEM((depth + 2 * columns, features), jnp.int16),
            pltpu.VMEM((depth, clips), jnp.int16),
            pltpu.VMEM((features, depth), jnp.bfloat16),
            pltpu.VMEM((features, depth), jnp.bfloat16),
            pltpu.VMEM((depth, clips), jnp.bfloat16),
            pltpu.VMEM((depth, clips), jnp.bfloat16),
            pltpu.SemaphoreType.DMA((len(freqs),)),
            pltpu.SemaphoreType.DMA((len(early),)),
        ],
        compiler_params=pltpu.CompilerParams(vmem_limit_bytes=EARLY_VMEM_BYTES),
        cost_estimate=pl.CostEstimate(
            flops=6 * features * depth * clips, bytes_accessed=8 * features * clips, transcendentals=0
        ),
        name="early_angles",
    )(jnp.stack([line, clip, core]).astype(jnp.int32), *early, *freqs)
    last, high = tie((own[3], high))
    phi = pl.pallas_call(
        functools.partial(late_kernel, columns=columns, scale=scale),
        out_shape=jax.ShapeDtypeStruct((features, clips), jnp.bfloat16),
        in_specs=[anywhere] * 3 + [vmem] * 3,
        out_specs=vmem,
        scratch_shapes=[
            pltpu.VMEM((features, clips), jnp.float32),
            pltpu.VMEM((2 * columns, clips), jnp.int16),
            pltpu.VMEM((2 * columns, clips), jnp.bfloat16),
            pltpu.VMEM((2 * columns, clips), jnp.bfloat16),
            pltpu.SemaphoreType.DMA((1,)),
            pltpu.SemaphoreType.DMA((2,)),
        ],
        compiler_params=pltpu.CompilerParams(vmem_limit_bytes=VMEM_BYTES),
        cost_estimate=pl.CostEstimate(
            flops=6 * features * 2 * columns * clips, bytes_accessed=6 * features * clips, transcendentals=0
        ),
        name="late_angles",
    )(summed, last, core_swap(last), high, low, column)
    return phi, rest


def phi_by_ring(embed_code, freq_code, column, scale, line, core, clip, prepare):
    places, n_clip = lax.axis_size("feat") // 2, lax.axis_size("clip")
    columns, clips = embed_code.shape
    slab, features = 2 * places * columns // n_clip, freq_code[0].shape[1]
    freqs = [y for k in range(n_clip) for y in (x if k == 0 else clip_swap(x, k) for x in freq_code)]
    freq_all = jnp.zeros((n_clip * slab, features), jnp.int16)
    for i, piece in enumerate(freqs):
        at = (clip ^ (i // 2)) * slab + (i % 2) * (slab // 2)
        freq_all = lax.dynamic_update_slice_in_dim(freq_all, piece[: slab // 2], at, 0)
    embed_all = jnp.zeros((2 * places * columns, clips), jnp.int16)
    piece = embed_code
    ring = [(i, (i + 1) % places) for i in range(places)]
    for step in range(places):
        if step:
            piece = line_move(piece, ring)
        base = 2 * ((line - step) % places)
        embed_all = lax.dynamic_update_slice_in_dim(embed_all, piece, (base + core) * columns, 0)
        embed_all = lax.dynamic_update_slice_in_dim(
            embed_all, core_swap(piece), (base + 1 - core) * columns, 0
        )

    def dot0(a, b):
        return lax.dot_general(a, b, (((0,), (0,)), ((), ())), preferred_element_type=jnp.float32)

    embed_high, embed_low = split(embed_all)
    freq_high, freq_low = split(freq_all)
    total = dot0(freq_high, embed_high) + (dot0(freq_high, embed_low) + dot0(freq_low, embed_high))
    return scaled_cos(total * PER_TURN + column, scale), prepare(freqs)


def per_device(embeds, frequencies, phases, weights, labels):
    n_feat, n_clip = lax.axis_size("feat"), lax.axis_size("clip")
    feat, clip = lax.axis_index("feat"), lax.axis_index("clip")
    places, line, core = n_feat // 2, feat // 2, feat % 2
    columns = embeds.shape[1]
    slab, features = frequencies.shape
    outputs = labels.shape[1]
    block = outputs // n_feat
    per_clip = places // n_clip
    scale = math.sqrt(2.0 / (features * n_feat))

    embed_code = encode(embeds.T, EMBED_BOUND)
    weight_rows = weights.T.reshape(per_clip, 2, block, features)
    freq_code = [
        jnp.concatenate(
            [
                encode(frequencies[h * (slab // 2) : (h + 1) * (slab // 2)], FREQ_BOUND),
                encode(weight_rows[:, h].reshape(-1, features), WEIGHT_BOUND),
            ]
        )
        for h in range(2)
    ]
    column = (phases * (0.5 / math.pi))[:, None]

    def prepare(codes):
        stacked = jnp.concatenate([code[slab // 2 :] for code in codes]).reshape(n_clip, 2, per_clip, block, features)

        def ordered(side):
            rows = lax.dynamic_index_in_dim(stacked, side, 1, keepdims=False).reshape(-1, block, features)
            found = []
            for k in range(places):
                place = line ^ k
                at = ((place // per_clip) ^ clip) * per_clip + place % per_clip
                found.append(lax.dynamic_index_in_dim(rows, at, 0, keepdims=False))
            return jnp.concatenate(found)

        def decode(code):
            return code.astype(jnp.float32) * (WEIGHT_BOUND / CODE_MAX)

        own, sent = lax.optimization_barrier((ordered(core), ordered(1 - core)))
        casts = lax.optimization_barrier((decode(own).astype(jnp.bfloat16), decode(sent).astype(jnp.bfloat16)))
        targets = lax.dynamic_slice_in_dim(labels.T, feat * block, block, 0).astype(jnp.float32)
        return decode(own), decode(core_swap(sent)), casts, targets

    def share_of(parts):
        parts = parts.reshape(places, block, -1)
        half = parts.astype(jnp.bfloat16)
        total = parts[0]
        found = [line_swap(half[k], k) for k in farthest_first(places)]
        return total, found

    def add_up(total, found):
        for x in found:
            total = total + x.astype(jnp.float32)
        return total

    def gradient_of(residual, phi):
        return lax.dot_general(residual, phi, (((1,), (1,)), ((), ())), preferred_element_type=jnp.float32)

    by_kernels = places == 4 and n_clip == 4 and columns % 16 == 0 and slab == 2 * columns
    phi_of = phi_by_kernels if by_kernels else phi_by_ring
    phi, (beta_own, beta_other, casts, targets) = phi_of(
        embed_code, freq_code, column, scale, line, core, clip, prepare
    )
    there = core_swap(mix(casts[1], phi).astype(jnp.bfloat16))
    parts = lax.optimization_barrier(mix(casts[0], phi)) + there.astype(jnp.float32)
    phi_other = core_swap(lax.optimization_barrier((phi, there))[0])
    moved_own = moved_other = 0.0
    for step in range(STEPS):
        share = (jax.nn.sigmoid(add_up(*share_of(parts))) - targets).astype(jnp.bfloat16)
        found = {k: line_swap(share, k) for k in farthest_first(places)}
        residual = jnp.concatenate([share] + [found[k] for k in range(1, places)])
        grad = jnp.concatenate([gradient_of(residual, phi), gradient_of(residual, phi_other)], axis=1)
        sent = grad.astype(jnp.bfloat16)
        for k in farthest_first(n_clip):
            grad = grad + clip_swap(sent, k).astype(jnp.float32)
        moved_own = moved_own + 0.25 * grad[:, :features]
        moved_other = moved_other + 0.25 * grad[:, features:]
        parts = mix((beta_own - moved_own).astype(jnp.bfloat16), phi) + mix(
            (beta_other - moved_other).astype(jnp.bfloat16), phi_other
        )
    total, found = share_of(parts)
    ours = moved_own.reshape(places, block, features)
    theirs = core_swap(moved_other).reshape(places, block, features)
    rows = []
    for b in range(per_clip):
        k = line ^ (clip * per_clip + b)
        mine = lax.dynamic_index_in_dim(ours, k, 0, keepdims=False)
        their = lax.dynamic_index_in_dim(theirs, k, 0, keepdims=False)
        rows += [jnp.where(core == 0, mine, their), jnp.where(core == 0, their, mine)]
    trained, total = lax.optimization_barrier((weights - jnp.concatenate(rows).T, total))
    return (trained, add_up(total, found).T)


def solution(mesh):
    placed = (P("clip", "feat"), P("clip", "feat"), P("feat"), P("feat", "clip"), P("clip", None))
    return jax.shard_map(
        per_device,
        mesh=mesh,
        in_specs=placed,
        out_specs=(P("feat", "clip"), P("clip", "feat")),
        check_vma=False,
    )
```

```python
import functools
import math

import jax
import jax.numpy as jnp
from jax import lax
from jax.experimental import pallas as pl
from jax.experimental.pallas import tpu as pltpu
from jax.sharding import PartitionSpec as P

STEPS = 2
EMBED_BOUND = 6.0
FREQ_BOUND = 0.5
CODE_MAX = 32766.0
LANES = 128
VMEM_BYTES = 16 * 1024 * 1024
EARLY_VMEM_BYTES = 56 * 1024 * 1024
WEIGHT_BOUND = 6.0
COS_TURNS = (
    0.9999999890590243,
    -19.739204499454,
    64.93911745989858,
    -85.45013953092679,
    60.16763095123224,
    -25.967599249288032,
    6.528658162158786,
)
PER_TURN = EMBED_BOUND * FREQ_BOUND / (CODE_MAX * CODE_MAX * 2.0 * math.pi)


def encode(x, bound):
    return jnp.round(x * (CODE_MAX / bound)).astype(jnp.int16)


def split(code):
    wide = code.astype(jnp.float32)
    high = jnp.round(wide * (1.0 / 256.0)) * 256.0
    return high.astype(jnp.bfloat16), (wide - high).astype(jnp.bfloat16)


def scaled_cos(turns, scale):
    turns = turns - jnp.round(turns)
    square = turns * turns
    value = COS_TURNS[-1] * scale
    for coefficient in COS_TURNS[-2::-1]:
        value = value * square + coefficient * scale
    return value.astype(jnp.bfloat16)


def mix(a, b):
    return jnp.dot(a, b, preferred_element_type=jnp.float32)


def core_swap(x):
    n = lax.axis_size("feat")
    return lax.ppermute(x, "feat", [(i, i ^ 1) for i in range(n)])


def line_swap(x, k):
    n = lax.axis_size("feat")
    return lax.ppermute(x, "feat", [(i, i ^ (2 * k)) for i in range(n)])


def line_move(x, pairs):
    return lax.ppermute(x, "feat", [(2 * a + c, 2 * b + c) for a, b in pairs for c in range(2)])


def clip_swap(x, k):
    n = lax.axis_size("clip")
    return lax.ppermute(x, "clip", [(i, i ^ k) for i in range(n)])


def farthest_first(n):
    return range(n - 1, 0, -1)


def halves(x):
    high = jnp.round(x * (1.0 / 256.0)) * 256.0
    return high.astype(jnp.bfloat16), (x - high).astype(jnp.bfloat16)


def early_kernel(at_ref, *refs, n_embeds, n_freqs, columns):
    embeds, freqs = refs[:n_embeds], refs[n_embeds : n_embeds + n_freqs]
    sum_ref, last_ref, freq_code, f_all, e_all = refs[n_embeds + n_freqs :]
    used = n_embeds * columns
    depth = e_all.shape[0] // 3

    @pl.when(pl.program_id(0) == 0)
    def _():
        line, clip, core = at_ref[0], at_ref[1], at_ref[2]

        def on_ring(place):
            return jnp.where(place == 0, 0, jnp.where(place == 1, 3, place - 1))

        for m in range(n_freqs // 2):
            step = (on_ring(line) - on_ring(clip ^ m)) & 3
            base = step * 2 * columns + jnp.where(step == 3, depth - used, 0)
            for h, side in enumerate((core, 1 - core)):
                row = pl.multiple_of(base + side * columns, 16)
                freq_code[pl.ds(row, columns), :] = freqs[2 * m + h][:columns, :]
        if depth > used:
            freq_code[used:depth, :] = jnp.zeros((depth - used, freq_code.shape[1]), jnp.int16)
            for start in range(0, 3 * depth, depth):
                e_all[start + used : start + depth, :] = jnp.zeros((depth - used, e_all.shape[1]), jnp.bfloat16)
        for start in range(0, depth, LANES):
            high, low = halves(freq_code[start : start + LANES, :].T.astype(jnp.float32))
            f_all[:, start : start + LANES] = high
            f_all[:, depth + start : depth + start + LANES] = high
            f_all[:, 2 * depth + start : 2 * depth + start + LANES] = low
        last_ref[0], last_ref[1] = halves(freq_code[depth:, :].T.astype(jnp.float32))

    for i, ref in enumerate(embeds):
        high, low = halves(ref[...].astype(jnp.float32))
        for start, value in ((0, high), (depth, low), (2 * depth, high)):
            e_all[start + i * columns : start + (i + 1) * columns, :] = value
    sum_ref[...] = mix(f_all[...], e_all[...])


def late_kernel(
    sum_ref, own_ref, other_ref, last_ref, phase_ref, beta_ref, phi_ref, keep_ref, send_ref, e_high, e_low, *, scale
):
    columns = own_ref.shape[0]
    for i, ref in enumerate((own_ref, other_ref)):
        rows = slice(i * columns, (i + 1) * columns)
        e_high[rows, :], e_low[rows, :] = halves(ref[...].astype(jnp.float32))
    total = sum_ref[...] + (
        mix(last_ref[0], e_high[...]) + (mix(last_ref[0], e_low[...]) + mix(last_ref[1], e_high[...]))
    )
    phi = scaled_cos(total * PER_TURN + phase_ref[...], scale)
    phi_ref[...] = phi
    logits = mix(beta_ref[...], phi)
    half = keep_ref.shape[0]
    keep_ref[...] = logits[:half]
    send_ref[...] = logits[half:].astype(jnp.bfloat16)


def phi_by_kernels(embed_code, freq_code, column, scale, line, core, clip, prepare):
    slabs = 4
    columns, clips = embed_code.shape
    features = freq_code[0].shape[1]
    tie = lax.optimization_barrier
    x_low, y_high = clip_swap(freq_code[0], 1), clip_swap(freq_code[1], 2)
    x_high, y_low = clip_swap(freq_code[1], 1), clip_swap(freq_code[0], 2)
    freqs = [*freq_code, x_low, x_high, y_low, y_high, clip_swap(x_low, 2), clip_swap(y_high, 1)]
    ring = [(0, 2), (2, 3), (3, 1), (1, 0)]
    own = [embed_code]
    for _ in range(slabs - 1):
        own.append(line_move(own[-1], ring))
    other = [core_swap(own[0]), core_swap(own[1])]
    *freqs, turn = tie((*freqs, own[2]))
    other.append(core_swap(turn))
    betas, cast = prepare(freqs)
    early = [x for pair in zip(own[:3], other) for x in pair]
    used = len(early) * columns
    depth = -(-used // LANES) * LANES
    tile = 256 if clips % 256 == 0 else clips

    def whole(*shape):
        return pl.BlockSpec(shape, lambda i: (0,) * len(shape))

    def by_clips(rows):
        return pl.BlockSpec((rows, tile), lambda i: (0, i))

    summed, freq_last = pl.pallas_call(
        functools.partial(early_kernel, n_embeds=len(early), n_freqs=len(freqs), columns=columns),
        grid=(clips // tile,),
        out_shape=(
            jax.ShapeDtypeStruct((features, clips), jnp.float32),
            jax.ShapeDtypeStruct((2, features, 2 * columns), jnp.bfloat16),
        ),
        in_specs=[pl.BlockSpec(memory_space=pltpu.SMEM)]
        + [by_clips(columns)] * len(early)
        + [whole(*x.shape) for x in freqs],
        out_specs=(by_clips(features), whole(2, features, 2 * columns)),
        scratch_shapes=[
            pltpu.VMEM((depth + 2 * columns, features), jnp.int16),
            pltpu.VMEM((features, 3 * depth), jnp.bfloat16),
            pltpu.VMEM((3 * depth, tile), jnp.bfloat16),
        ],
        compiler_params=pltpu.CompilerParams(vmem_limit_bytes=EARLY_VMEM_BYTES),
        cost_estimate=pl.CostEstimate(
            flops=6 * features * depth * clips, bytes_accessed=8 * features * clips, transcendentals=0
        ),
        name="early_angles",
    )(jnp.stack([line, clip, core]).astype(jnp.int32), *early, *freqs)
    last, freq_last = tie((own[3], freq_last))
    outputs = cast.shape[0]
    phi, keep, send = pl.pallas_call(
        functools.partial(late_kernel, scale=scale),
        grid=(clips // tile,),
        out_shape=(
            jax.ShapeDtypeStruct((features, clips), jnp.bfloat16),
            jax.ShapeDtypeStruct((outputs // 2, clips), jnp.float32),
            jax.ShapeDtypeStruct((outputs // 2, clips), jnp.bfloat16),
        ),
        in_specs=[
            by_clips(features),
            by_clips(columns),
            by_clips(columns),
            whole(2, features, 2 * columns),
            whole(features, 1),
            whole(outputs, features),
        ],
        out_specs=(by_clips(features), by_clips(outputs // 2), by_clips(outputs // 2)),
        scratch_shapes=[pltpu.VMEM((2 * columns, tile), jnp.bfloat16)] * 2,
        compiler_params=pltpu.CompilerParams(vmem_limit_bytes=VMEM_BYTES),
        cost_estimate=pl.CostEstimate(
            flops=6 * features * 2 * columns * clips, bytes_accessed=6 * features * clips, transcendentals=0
        ),
        name="late_angles",
    )(summed, last, core_swap(last), freq_last, column, cast)
    return phi, keep, send, betas


def phi_by_ring(embed_code, freq_code, column, scale, line, core, clip, prepare):
    places, n_clip = lax.axis_size("feat") // 2, lax.axis_size("clip")
    columns, clips = embed_code.shape
    slab, features = 2 * places * columns // n_clip, freq_code[0].shape[1]
    freqs = [y for k in range(n_clip) for y in (x if k == 0 else clip_swap(x, k) for x in freq_code)]
    freq_all = jnp.zeros((n_clip * slab, features), jnp.int16)
    for i, piece in enumerate(freqs):
        at = (clip ^ (i // 2)) * slab + (i % 2) * (slab // 2)
        freq_all = lax.dynamic_update_slice_in_dim(freq_all, piece[: slab // 2], at, 0)
    embed_all = jnp.zeros((2 * places * columns, clips), jnp.int16)
    piece = embed_code
    ring = [(i, (i + 1) % places) for i in range(places)]
    for step in range(places):
        if step:
            piece = line_move(piece, ring)
        base = 2 * ((line - step) % places)
        embed_all = lax.dynamic_update_slice_in_dim(embed_all, piece, (base + core) * columns, 0)
        embed_all = lax.dynamic_update_slice_in_dim(
            embed_all, core_swap(piece), (base + 1 - core) * columns, 0
        )

    def dot0(a, b):
        return lax.dot_general(a, b, (((0,), (0,)), ((), ())), preferred_element_type=jnp.float32)

    embed_high, embed_low = split(embed_all)
    freq_high, freq_low = split(freq_all)
    total = dot0(freq_high, embed_high) + (dot0(freq_high, embed_low) + dot0(freq_low, embed_high))
    phi = scaled_cos(total * PER_TURN + column, scale)
    betas, cast = prepare(freqs)
    logits = mix(cast, phi)
    half = logits.shape[0] // 2
    return phi, logits[:half], logits[half:].astype(jnp.bfloat16), betas


def per_device(embeds, frequencies, phases, weights, labels):
    n_feat, n_clip = lax.axis_size("feat"), lax.axis_size("clip")
    feat, clip = lax.axis_index("feat"), lax.axis_index("clip")
    places, line, core = n_feat // 2, feat // 2, feat % 2
    columns = embeds.shape[1]
    slab, features = frequencies.shape
    outputs = labels.shape[1]
    block = outputs // n_feat
    per_clip = places // n_clip
    scale = math.sqrt(2.0 / (features * n_feat))

    embed_code = encode(embeds.T, EMBED_BOUND)
    weight_rows = weights.T.reshape(per_clip, 2, block, features)
    freq_code = [
        jnp.concatenate(
            [
                encode(frequencies[h * (slab // 2) : (h + 1) * (slab // 2)], FREQ_BOUND),
                encode(weight_rows[:, h].reshape(-1, features), WEIGHT_BOUND),
            ]
        )
        for h in range(2)
    ]
    column = (phases * (0.5 / math.pi))[:, None]

    def prepare(codes):
        stacked = jnp.concatenate([code[slab // 2 :] for code in codes]).reshape(n_clip, 2, per_clip, block, features)

        def ordered(side):
            rows = lax.dynamic_index_in_dim(stacked, side, 1, keepdims=False).reshape(-1, block, features)
            found = []
            for k in range(places):
                place = line ^ k
                at = ((place // per_clip) ^ clip) * per_clip + place % per_clip
                found.append(lax.dynamic_index_in_dim(rows, at, 0, keepdims=False))
            return jnp.concatenate(found)

        def decode(code):
            return code.astype(jnp.float32) * (WEIGHT_BOUND / CODE_MAX)

        own, sent = lax.optimization_barrier((ordered(core), ordered(1 - core)))
        cast = lax.optimization_barrier(decode(jnp.concatenate([own, sent])).astype(jnp.bfloat16))
        return (decode(own), decode(core_swap(sent))), cast

    def share_of(parts):
        parts = parts.reshape(places, block, -1)
        half = parts.astype(jnp.bfloat16)
        total = parts[0]
        found = [line_swap(half[k], k) for k in farthest_first(places)]
        return total, found

    def add_up(total, found):
        for x in found:
            total = total + x.astype(jnp.float32)
        return total

    def gradient_of(residual, phi):
        return lax.dot_general(residual, phi, (((1,), (1,)), ((), ())), preferred_element_type=jnp.float32)

    by_kernels = places == 4 and n_clip == 4 and columns % 16 == 0 and slab == 2 * columns
    phi_of = phi_by_kernels if by_kernels else phi_by_ring
    phi, keep, send, (beta_own, beta_other) = phi_of(
        embed_code, freq_code, column, scale, line, core, clip, prepare
    )
    targets = lax.dynamic_slice_in_dim(labels.T, feat * block, block, 0).astype(jnp.float32)
    there = core_swap(send)
    parts = keep + there.astype(jnp.float32)
    phi_other = core_swap(lax.optimization_barrier((phi, there))[0])
    phi_both = lax.optimization_barrier(jnp.concatenate([phi, phi_other]))
    beta = jnp.concatenate([beta_own, beta_other], axis=1)
    moved = 0.0
    for step in range(STEPS):
        share = (jax.nn.sigmoid(add_up(*share_of(parts))) - targets).astype(jnp.bfloat16)
        found = {k: line_swap(share, k) for k in farthest_first(places)}
        residual = jnp.concatenate([share] + [found[k] for k in range(1, places)])
        grad = gradient_of(residual, phi_both)
        sent = grad.astype(jnp.bfloat16)
        for k in farthest_first(n_clip):
            grad = grad + clip_swap(sent, k).astype(jnp.float32)
        moved = moved + 0.25 * grad
        cast = lax.optimization_barrier((beta - moved).astype(jnp.bfloat16))
        parts = mix(cast, phi_both)
    total, found = share_of(parts)
    ours = moved[:, :features].reshape(places, block, features)
    theirs = core_swap(moved[:, features:]).reshape(places, block, features)
    rows = []
    for b in range(per_clip):
        k = line ^ (clip * per_clip + b)
        mine = lax.dynamic_index_in_dim(ours, k, 0, keepdims=False)
        their = lax.dynamic_index_in_dim(theirs, k, 0, keepdims=False)
        rows += [jnp.where(core == 0, mine, their), jnp.where(core == 0, their, mine)]
    trained, total = lax.optimization_barrier((weights - jnp.concatenate(rows).T, total))
    return (trained, add_up(total, found).T)


def solution(mesh):
    placed = (P("clip", "feat"), P("clip", "feat"), P("feat"), P("feat", "clip"), P("clip", None))
    return jax.shard_map(
        per_device,
        mesh=mesh,
        in_specs=placed,
        out_specs=(P("feat", "clip"), P("clip", "feat")),
        check_vma=False,
    )
```

```python
import functools
import math

import jax
import jax.numpy as jnp
from jax import lax
from jax.experimental import pallas as pl
from jax.experimental.pallas import tpu as pltpu
from jax.sharding import PartitionSpec as P

STEPS = 2
EMBED_BOUND = 6.0
FREQ_BOUND = 0.5
CODE_MAX = 32766.0
LANES = 128
VMEM_BYTES = 16 * 1024 * 1024
EARLY_VMEM_BYTES = 36 * 1024 * 1024
WEIGHT_BOUND = 6.0
COS_TURNS = (
    0.9999999890590243,
    -19.739204499454,
    64.93911745989858,
    -85.45013953092679,
    60.16763095123224,
    -25.967599249288032,
    6.528658162158786,
)
PER_TURN = EMBED_BOUND * FREQ_BOUND / (CODE_MAX * CODE_MAX * 2.0 * math.pi)


def encode(x, bound):
    return jnp.round(x * (CODE_MAX / bound)).astype(jnp.int16)


def split(code):
    wide = code.astype(jnp.float32)
    high = jnp.round(wide * (1.0 / 256.0)) * 256.0
    return high.astype(jnp.bfloat16), (wide - high).astype(jnp.bfloat16)


def scaled_cos(turns, scale):
    turns = turns - jnp.round(turns)
    square = turns * turns
    value = COS_TURNS[-1] * scale
    for coefficient in COS_TURNS[-2::-1]:
        value = value * square + coefficient * scale
    return value.astype(jnp.bfloat16)


def mix(a, b):
    return jnp.dot(a, b, preferred_element_type=jnp.float32)


def core_swap(x):
    n = lax.axis_size("feat")
    return lax.ppermute(x, "feat", [(i, i ^ 1) for i in range(n)])


def line_swap(x, k):
    n = lax.axis_size("feat")
    return lax.ppermute(x, "feat", [(i, i ^ (2 * k)) for i in range(n)])


def line_move(x, pairs):
    return lax.ppermute(x, "feat", [(2 * a + c, 2 * b + c) for a, b in pairs for c in range(2)])


def clip_swap(x, k):
    n = lax.axis_size("clip")
    return lax.ppermute(x, "clip", [(i, i ^ k) for i in range(n)])


def farthest_first(n):
    return range(n - 1, 0, -1)


def halves(x):
    high = jnp.round(x * (1.0 / 256.0)) * 256.0
    return high.astype(jnp.bfloat16), (x - high).astype(jnp.bfloat16)


def early_kernel(at_ref, *refs, n_embeds, n_freqs, columns):
    embeds, freqs = refs[:n_embeds], refs[n_embeds : n_embeds + n_freqs]
    sum_ref, last_ref, freq_code, f_all, e_all = refs[n_embeds + n_freqs :]
    used = n_embeds * columns
    depth = e_all.shape[0] // 3

    @pl.when(pl.program_id(0) == 0)
    def _():
        line, clip, core = at_ref[0], at_ref[1], at_ref[2]

        def on_ring(place):
            return jnp.where(place == 0, 0, jnp.where(place == 1, 3, place - 1))

        for m in range(n_freqs // 2):
            step = (on_ring(line) - on_ring(clip ^ m)) & 3
            base = step * 2 * columns + jnp.where(step == 3, depth - used, 0)
            for h, side in enumerate((core, 1 - core)):
                row = pl.multiple_of(base + side * columns, 16)
                freq_code[pl.ds(row, columns), :] = freqs[2 * m + h][:columns, :]
        if depth > used:
            freq_code[used:depth, :] = jnp.zeros((depth - used, freq_code.shape[1]), jnp.int16)
            for start in range(0, 3 * depth, depth):
                e_all[start + used : start + depth, :] = jnp.zeros((depth - used, e_all.shape[1]), jnp.bfloat16)
        for start in range(0, depth, LANES):
            high, low = halves(freq_code[start : start + LANES, :].T.astype(jnp.float32))
            f_all[:, start : start + LANES] = high
            f_all[:, depth + start : depth + start + LANES] = high
            f_all[:, 2 * depth + start : 2 * depth + start + LANES] = low
        last_ref[...] = freq_code[depth:, :].T

    for i, ref in enumerate(embeds):
        high, low = halves(ref[...].astype(jnp.float32))
        for start, value in ((0, high), (depth, low), (2 * depth, high)):
            e_all[start + i * columns : start + (i + 1) * columns, :] = value
    sum_ref[...] = mix(f_all[...], e_all[...])


def late_kernel(
    sum_ref, own_ref, other_ref, last_ref, phase_ref, beta_ref, phi_ref, keep_ref, send_ref, e_all, f_all, *, scale
):
    columns = own_ref.shape[0]
    depth = 2 * columns
    for i, ref in enumerate((own_ref, other_ref)):
        high, low = halves(ref[...].astype(jnp.float32))
        for start, value in ((0, high), (depth, low), (2 * depth, high)):
            e_all[start + i * columns : start + (i + 1) * columns, :] = value

    @pl.when(pl.program_id(0) == 0)
    def _():
        high, low = halves(last_ref[...].astype(jnp.float32))
        f_all[:, :depth], f_all[:, depth : 2 * depth], f_all[:, 2 * depth :] = high, high, low

    total = sum_ref[...] + mix(f_all[...], e_all[...])
    phi = scaled_cos(total * PER_TURN + phase_ref[...], scale)
    phi_ref[...] = phi
    logits = mix(beta_ref[...], phi)
    half = keep_ref.shape[0]
    keep_ref[...] = logits[:half]
    send_ref[...] = logits[half:].astype(jnp.bfloat16)


def phi_by_kernels(embed_code, freq_code, column, scale, line, core, clip, prepare):
    slabs = 4
    columns, clips = embed_code.shape
    features = freq_code[0].shape[1]
    tie = lax.optimization_barrier
    x_low, y_high = clip_swap(freq_code[0], 1), clip_swap(freq_code[1], 2)
    x_high, y_low = clip_swap(freq_code[1], 1), clip_swap(freq_code[0], 2)
    freqs = [*freq_code, x_low, x_high, y_low, y_high, clip_swap(x_low, 2), clip_swap(y_high, 1)]
    ring = [(0, 2), (2, 3), (3, 1), (1, 0)]
    own = [embed_code]
    for _ in range(slabs - 1):
        own.append(line_move(own[-1], ring))
    other = [core_swap(own[0]), core_swap(own[1])]
    *freqs, turn = tie((*freqs, own[2]))
    other.append(core_swap(turn))
    betas, cast = prepare(freqs)
    early = [x for pair in zip(own[:3], other) for x in pair]
    used = len(early) * columns
    depth = -(-used // LANES) * LANES
    tile = 512 if clips % 512 == 0 else clips

    def whole(*shape):
        return pl.BlockSpec(shape, lambda i: (0,) * len(shape))

    def by_clips(rows):
        return pl.BlockSpec((rows, tile), lambda i: (0, i))

    summed, freq_last = pl.pallas_call(
        functools.partial(early_kernel, n_embeds=len(early), n_freqs=len(freqs), columns=columns),
        grid=(clips // tile,),
        out_shape=(
            jax.ShapeDtypeStruct((features, clips), jnp.float32),
            jax.ShapeDtypeStruct((features, 2 * columns), jnp.int16),
        ),
        in_specs=[pl.BlockSpec(memory_space=pltpu.SMEM)]
        + [by_clips(columns)] * len(early)
        + [whole(*x.shape) for x in freqs],
        out_specs=(by_clips(features), whole(features, 2 * columns)),
        scratch_shapes=[
            pltpu.VMEM((depth + 2 * columns, features), jnp.int16),
            pltpu.VMEM((features, 3 * depth), jnp.bfloat16),
            pltpu.VMEM((3 * depth, tile), jnp.bfloat16),
        ],
        compiler_params=pltpu.CompilerParams(vmem_limit_bytes=EARLY_VMEM_BYTES),
        cost_estimate=pl.CostEstimate(
            flops=6 * features * depth * clips, bytes_accessed=8 * features * clips, transcendentals=0
        ),
        name="early_angles",
    )(jnp.stack([line, clip, core]).astype(jnp.int32), *early, *freqs)
    last, freq_last = tie((own[3], freq_last))
    outputs = cast.shape[0]
    phi, keep, send = pl.pallas_call(
        functools.partial(late_kernel, scale=scale),
        grid=(clips // tile,),
        out_shape=(
            jax.ShapeDtypeStruct((features, clips), jnp.bfloat16),
            jax.ShapeDtypeStruct((outputs // 2, clips), jnp.float32),
            jax.ShapeDtypeStruct((outputs // 2, clips), jnp.bfloat16),
        ),
        in_specs=[
            by_clips(features),
            by_clips(columns),
            by_clips(columns),
            whole(features, 2 * columns),
            whole(features, 1),
            whole(outputs, features),
        ],
        out_specs=(by_clips(features), by_clips(outputs // 2), by_clips(outputs // 2)),
        scratch_shapes=[
            pltpu.VMEM((6 * columns, tile), jnp.bfloat16),
            pltpu.VMEM((features, 6 * columns), jnp.bfloat16),
        ],
        compiler_params=pltpu.CompilerParams(vmem_limit_bytes=VMEM_BYTES),
        cost_estimate=pl.CostEstimate(
            flops=6 * features * 2 * columns * clips, bytes_accessed=6 * features * clips, transcendentals=0
        ),
        name="late_angles",
    )(summed, last, core_swap(last), freq_last, column, cast)
    return phi, keep, send, betas


def phi_by_ring(embed_code, freq_code, column, scale, line, core, clip, prepare):
    places, n_clip = lax.axis_size("feat") // 2, lax.axis_size("clip")
    columns, clips = embed_code.shape
    slab, features = 2 * places * columns // n_clip, freq_code[0].shape[1]
    freqs = [y for k in range(n_clip) for y in (x if k == 0 else clip_swap(x, k) for x in freq_code)]
    freq_all = jnp.zeros((n_clip * slab, features), jnp.int16)
    for i, piece in enumerate(freqs):
        at = (clip ^ (i // 2)) * slab + (i % 2) * (slab // 2)
        freq_all = lax.dynamic_update_slice_in_dim(freq_all, piece[: slab // 2], at, 0)
    embed_all = jnp.zeros((2 * places * columns, clips), jnp.int16)
    piece = embed_code
    ring = [(i, (i + 1) % places) for i in range(places)]
    for step in range(places):
        if step:
            piece = line_move(piece, ring)
        base = 2 * ((line - step) % places)
        embed_all = lax.dynamic_update_slice_in_dim(embed_all, piece, (base + core) * columns, 0)
        embed_all = lax.dynamic_update_slice_in_dim(
            embed_all, core_swap(piece), (base + 1 - core) * columns, 0
        )

    def dot0(a, b):
        return lax.dot_general(a, b, (((0,), (0,)), ((), ())), preferred_element_type=jnp.float32)

    embed_high, embed_low = split(embed_all)
    freq_high, freq_low = split(freq_all)
    total = dot0(freq_high, embed_high) + (dot0(freq_high, embed_low) + dot0(freq_low, embed_high))
    phi = scaled_cos(total * PER_TURN + column, scale)
    betas, cast = prepare(freqs)
    logits = mix(cast, phi)
    half = logits.shape[0] // 2
    return phi, logits[:half], logits[half:].astype(jnp.bfloat16), betas


def per_device(embeds, frequencies, phases, weights, labels):
    n_feat, n_clip = lax.axis_size("feat"), lax.axis_size("clip")
    feat, clip = lax.axis_index("feat"), lax.axis_index("clip")
    places, line, core = n_feat // 2, feat // 2, feat % 2
    columns = embeds.shape[1]
    slab, features = frequencies.shape
    outputs = labels.shape[1]
    block = outputs // n_feat
    per_clip = places // n_clip
    scale = math.sqrt(2.0 / (features * n_feat))

    embed_code = encode(embeds.T, EMBED_BOUND)
    weight_rows = weights.T.reshape(per_clip, 2, block, features)
    freq_code = [
        jnp.concatenate(
            [
                encode(frequencies[h * (slab // 2) : (h + 1) * (slab // 2)], FREQ_BOUND),
                encode(weight_rows[:, h].reshape(-1, features), WEIGHT_BOUND),
            ]
        )
        for h in range(2)
    ]
    column = (phases * (0.5 / math.pi))[:, None]

    def prepare(codes):
        stacked = jnp.concatenate([code[slab // 2 :] for code in codes]).reshape(n_clip, 2, per_clip, block, features)

        def ordered(side):
            rows = lax.dynamic_index_in_dim(stacked, side, 1, keepdims=False).reshape(-1, block, features)
            found = []
            for k in range(places):
                place = line ^ ((places - k) % places)
                at = ((place // per_clip) ^ clip) * per_clip + place % per_clip
                found.append(lax.dynamic_index_in_dim(rows, at, 0, keepdims=False))
            return jnp.concatenate(found)

        def decode(code):
            return code.astype(jnp.float32) * (WEIGHT_BOUND / CODE_MAX)

        own, sent = lax.optimization_barrier((ordered(core), ordered(1 - core)))
        cast = lax.optimization_barrier(decode(jnp.concatenate([own, sent])).astype(jnp.bfloat16))
        return (decode(own), decode(core_swap(sent))), cast

    def share_of(parts):
        parts = parts.reshape(places, block, -1)
        half = parts.astype(jnp.bfloat16)
        total = parts[0]
        found = [line_swap(half[k], places - k) for k in range(1, places)]
        return total, found

    def add_up(total, found):
        for x in found:
            total = total + x.astype(jnp.float32)
        return total

    def gradient_of(residual, phi):
        return lax.dot_general(residual, phi, (((1,), (1,)), ((), ())), preferred_element_type=jnp.float32)

    by_kernels = places == 4 and n_clip == 4 and columns % 16 == 0 and slab == 2 * columns
    phi_of = phi_by_kernels if by_kernels else phi_by_ring
    phi, keep, send, (beta_own, beta_other) = phi_of(
        embed_code, freq_code, column, scale, line, core, clip, prepare
    )
    targets = lax.dynamic_slice_in_dim(labels.T, feat * block, block, 0).astype(jnp.float32)
    there = core_swap(send)
    parts = keep + there.astype(jnp.float32)
    phi_other = core_swap(lax.optimization_barrier((phi, there))[0])
    phi_both = lax.optimization_barrier(jnp.concatenate([phi, phi_other]))
    beta = jnp.concatenate([beta_own, beta_other], axis=1)
    moved = 0.0
    for step in range(STEPS):
        share = (jax.nn.sigmoid(add_up(*share_of(parts))) - targets).astype(jnp.bfloat16)
        residual = jnp.concatenate([share] + [line_swap(share, places - k) for k in range(1, places)])
        grad = gradient_of(residual, phi_both)
        sent = grad.astype(jnp.bfloat16)
        for k in farthest_first(n_clip):
            grad = grad + clip_swap(sent, k).astype(jnp.float32)
        moved = moved + 0.25 * grad
        cast = lax.optimization_barrier((beta - moved).astype(jnp.bfloat16))
        parts = mix(cast, phi_both)
    total, found = share_of(parts)
    ours = moved[:, :features].reshape(places, block, features)
    theirs = core_swap(moved[:, features:]).reshape(places, block, features)
    rows = []
    for b in range(per_clip):
        k = (places - (line ^ (clip * per_clip + b))) % places
        mine = lax.dynamic_index_in_dim(ours, k, 0, keepdims=False)
        their = lax.dynamic_index_in_dim(theirs, k, 0, keepdims=False)
        rows += [jnp.where(core == 0, mine, their), jnp.where(core == 0, their, mine)]
    trained, total = lax.optimization_barrier((weights - jnp.concatenate(rows).T, total))
    return (trained, add_up(total, found).T)


def solution(mesh):
    placed = (P("clip", "feat"), P("clip", "feat"), P("feat"), P("feat", "clip"), P("clip", None))
    return jax.shard_map(
        per_device,
        mesh=mesh,
        in_specs=placed,
        out_specs=(P("feat", "clip"), P("clip", "feat")),
        check_vma=False,
    )
```

```python
import functools
import math

import jax
import jax.numpy as jnp
from jax import lax
from jax.experimental import pallas as pl
from jax.experimental.pallas import tpu as pltpu
from jax.sharding import PartitionSpec as P

STEPS = 2
EMBED_BOUND = 6.0
FREQ_BOUND = 0.5
CODE_MAX = 32766.0
LANES = 128
VMEM_BYTES = 16 * 1024 * 1024
EARLY_VMEM_BYTES = 36 * 1024 * 1024
WEIGHT_BOUND = 6.0
COS_TURNS = (
    0.9999999890590243,
    -19.739204499454,
    64.93911745989858,
    -85.45013953092679,
    60.16763095123224,
    -25.967599249288032,
    6.528658162158786,
)
PER_TURN = EMBED_BOUND * FREQ_BOUND / (CODE_MAX * CODE_MAX * 2.0 * math.pi)


def encode(x, bound):
    return jnp.round(x * (CODE_MAX / bound)).astype(jnp.int16)


def split(code):
    wide = code.astype(jnp.float32)
    high = jnp.round(wide * (1.0 / 256.0)) * 256.0
    return high.astype(jnp.bfloat16), (wide - high).astype(jnp.bfloat16)


def scaled_cos(turns, scale):
    turns = turns - jnp.round(turns)
    square = turns * turns
    value = COS_TURNS[-1] * scale
    for coefficient in COS_TURNS[-2::-1]:
        value = value * square + coefficient * scale
    return value.astype(jnp.bfloat16)


def mix(a, b):
    return jnp.dot(a, b, preferred_element_type=jnp.float32)


def core_swap(x):
    n = lax.axis_size("feat")
    return lax.ppermute(x, "feat", [(i, i ^ 1) for i in range(n)])


def line_swap(x, k):
    n = lax.axis_size("feat")
    return lax.ppermute(x, "feat", [(i, i ^ (2 * k)) for i in range(n)])


def line_move(x, pairs):
    return lax.ppermute(x, "feat", [(2 * a + c, 2 * b + c) for a, b in pairs for c in range(2)])


def clip_swap(x, k):
    n = lax.axis_size("clip")
    return lax.ppermute(x, "clip", [(i, i ^ k) for i in range(n)])


def farthest_first(n):
    return range(n - 1, 0, -1)


def halves(x):
    high = jnp.round(x * (1.0 / 256.0)) * 256.0
    return high.astype(jnp.bfloat16), (x - high).astype(jnp.bfloat16)


def early_kernel(at_ref, *refs, n_embeds, n_freqs, columns):
    embeds, freqs = refs[:n_embeds], refs[n_embeds : n_embeds + n_freqs]
    sum_ref, last_ref, freq_code, f_all, e_all = refs[n_embeds + n_freqs :]
    used = n_embeds * columns
    depth = e_all.shape[0] // 3

    @pl.when(pl.program_id(0) == 0)
    def _():
        line, clip, core = at_ref[0], at_ref[1], at_ref[2]

        def on_ring(place):
            return jnp.where(place == 0, 0, jnp.where(place == 1, 3, place - 1))

        rows = freqs[-1].shape[0]
        pieces = [(ref, h * rows) for ref in freqs[:-2] for h in range(2)] + [(ref, 0) for ref in freqs[-2:]]
        for m in range(len(pieces) // 2):
            step = (on_ring(line) - on_ring(clip ^ m)) & 3
            base = step * 2 * columns + jnp.where(step == 3, depth - used, 0)
            for (ref, start), side in zip(pieces[2 * m : 2 * m + 2], (core, 1 - core)):
                row = pl.multiple_of(base + side * columns, 16)
                freq_code[pl.ds(row, columns), :] = ref[start : start + columns, :]
        if depth > used:
            freq_code[used:depth, :] = jnp.zeros((depth - used, freq_code.shape[1]), jnp.int16)
            for start in range(0, 3 * depth, depth):
                e_all[start + used : start + depth, :] = jnp.zeros((depth - used, e_all.shape[1]), jnp.bfloat16)
        for start in range(0, depth, LANES):
            high, low = halves(freq_code[start : start + LANES, :].T.astype(jnp.float32))
            f_all[:, start : start + LANES] = high
            f_all[:, depth + start : depth + start + LANES] = high
            f_all[:, 2 * depth + start : 2 * depth + start + LANES] = low
        last_ref[...] = freq_code[depth:, :].T

    for i, ref in enumerate(embeds):
        high, low = halves(ref[...].astype(jnp.float32))
        for start, value in ((0, high), (depth, low), (2 * depth, high)):
            e_all[start + i * columns : start + (i + 1) * columns, :] = value
    sum_ref[...] = mix(f_all[...], e_all[...])


def late_kernel(
    sum_ref, own_ref, other_ref, last_ref, phase_ref, beta_ref, phi_ref, keep_ref, send_ref, e_all, f_all, *, scale
):
    columns = own_ref.shape[0]
    depth = 2 * columns
    for i, ref in enumerate((own_ref, other_ref)):
        high, low = halves(ref[...].astype(jnp.float32))
        for start, value in ((0, high), (depth, low), (2 * depth, high)):
            e_all[start + i * columns : start + (i + 1) * columns, :] = value

    @pl.when(pl.program_id(0) == 0)
    def _():
        high, low = halves(last_ref[...].astype(jnp.float32))
        f_all[:, :depth], f_all[:, depth : 2 * depth], f_all[:, 2 * depth :] = high, high, low

    total = sum_ref[...] + mix(f_all[...], e_all[...])
    phi = scaled_cos(total * PER_TURN + phase_ref[...], scale)
    phi_ref[...] = phi
    logits = mix(beta_ref[...], phi)
    half = keep_ref.shape[0]
    keep_ref[...] = logits[:half]
    send_ref[...] = logits[half:].astype(jnp.bfloat16)


def phi_by_kernels(embed_code, freq_code, column, scale, line, core, clip, prepare):
    slabs = 4
    columns, clips = embed_code.shape
    features = freq_code.shape[1]
    tie = lax.optimization_barrier
    rows = freq_code.shape[0] // 2
    freq_x, freq_y = clip_swap(freq_code, 1), clip_swap(freq_code, 2)
    ring = [(0, 2), (2, 3), (3, 1), (1, 0)]
    own = [embed_code]
    for _ in range(slabs - 1):
        own.append(line_move(own[-1], ring))
    other = [core_swap(own[0]), core_swap(own[1])]
    x_again, y_again, other[1] = tie((freq_x, freq_y, other[1]))
    freqs = [freq_code, freq_x, freq_y, clip_swap(x_again[:rows], 2), clip_swap(y_again[rows:], 1)]
    other.append(core_swap(own[2]))
    *freqs, own[2] = tie((*freqs, own[2]))
    betas, cast = prepare(freqs)
    early = [x for pair in zip(own[:3], other) for x in pair]
    used = len(early) * columns
    depth = -(-used // LANES) * LANES
    tile = 512 if clips % 512 == 0 else clips

    def whole(*shape):
        return pl.BlockSpec(shape, lambda i: (0,) * len(shape))

    def by_clips(rows):
        return pl.BlockSpec((rows, tile), lambda i: (0, i))

    summed, freq_last = pl.pallas_call(
        functools.partial(early_kernel, n_embeds=len(early), n_freqs=len(freqs), columns=columns),
        grid=(clips // tile,),
        out_shape=(
            jax.ShapeDtypeStruct((features, clips), jnp.float32),
            jax.ShapeDtypeStruct((features, 2 * columns), jnp.int16),
        ),
        in_specs=[pl.BlockSpec(memory_space=pltpu.SMEM)]
        + [by_clips(columns)] * len(early)
        + [whole(*x.shape) for x in freqs],
        out_specs=(by_clips(features), whole(features, 2 * columns)),
        scratch_shapes=[
            pltpu.VMEM((depth + 2 * columns, features), jnp.int16),
            pltpu.VMEM((features, 3 * depth), jnp.bfloat16),
            pltpu.VMEM((3 * depth, tile), jnp.bfloat16),
        ],
        compiler_params=pltpu.CompilerParams(vmem_limit_bytes=EARLY_VMEM_BYTES),
        cost_estimate=pl.CostEstimate(
            flops=6 * features * depth * clips, bytes_accessed=8 * features * clips, transcendentals=0
        ),
        name="early_angles",
    )(jnp.stack([line, clip, core]).astype(jnp.int32), *early, *freqs)
    last, freq_last = tie((own[3], freq_last))
    outputs = cast.shape[0]
    phi, keep, send = pl.pallas_call(
        functools.partial(late_kernel, scale=scale),
        grid=(clips // tile,),
        out_shape=(
            jax.ShapeDtypeStruct((features, clips), jnp.bfloat16),
            jax.ShapeDtypeStruct((outputs // 2, clips), jnp.float32),
            jax.ShapeDtypeStruct((outputs // 2, clips), jnp.bfloat16),
        ),
        in_specs=[
            by_clips(features),
            by_clips(columns),
            by_clips(columns),
            whole(features, 2 * columns),
            whole(features, 1),
            whole(outputs, features),
        ],
        out_specs=(by_clips(features), by_clips(outputs // 2), by_clips(outputs // 2)),
        scratch_shapes=[
            pltpu.VMEM((6 * columns, tile), jnp.bfloat16),
            pltpu.VMEM((features, 6 * columns), jnp.bfloat16),
        ],
        compiler_params=pltpu.CompilerParams(vmem_limit_bytes=VMEM_BYTES),
        cost_estimate=pl.CostEstimate(
            flops=6 * features * 2 * columns * clips, bytes_accessed=6 * features * clips, transcendentals=0
        ),
        name="late_angles",
    )(summed, last, core_swap(last), freq_last, column, cast)
    return phi, keep, send, betas


def phi_by_ring(embed_code, freq_code, column, scale, line, core, clip, prepare):
    places, n_clip = lax.axis_size("feat") // 2, lax.axis_size("clip")
    columns, clips = embed_code.shape
    slab, features = 2 * places * columns // n_clip, freq_code.shape[1]
    freqs = [freq_code] + [clip_swap(freq_code, k) for k in range(1, n_clip)]
    freq_all = jnp.zeros((n_clip * slab, features), jnp.int16)
    for k, piece in enumerate(freqs):
        for h in range(2):
            half = piece[h * (piece.shape[0] // 2) :][: slab // 2]
            freq_all = lax.dynamic_update_slice_in_dim(freq_all, half, (clip ^ k) * slab + h * (slab // 2), 0)
    embed_all = jnp.zeros((2 * places * columns, clips), jnp.int16)
    piece = embed_code
    ring = [(i, (i + 1) % places) for i in range(places)]
    for step in range(places):
        if step:
            piece = line_move(piece, ring)
        base = 2 * ((line - step) % places)
        embed_all = lax.dynamic_update_slice_in_dim(embed_all, piece, (base + core) * columns, 0)
        embed_all = lax.dynamic_update_slice_in_dim(
            embed_all, core_swap(piece), (base + 1 - core) * columns, 0
        )

    def dot0(a, b):
        return lax.dot_general(a, b, (((0,), (0,)), ((), ())), preferred_element_type=jnp.float32)

    embed_high, embed_low = split(embed_all)
    freq_high, freq_low = split(freq_all)
    total = dot0(freq_high, embed_high) + (dot0(freq_high, embed_low) + dot0(freq_low, embed_high))
    phi = scaled_cos(total * PER_TURN + column, scale)
    betas, cast = prepare(freqs)
    logits = mix(cast, phi)
    half = logits.shape[0] // 2
    return phi, logits[:half], logits[half:].astype(jnp.bfloat16), betas


def per_device(embeds, frequencies, phases, weights, labels):
    n_feat, n_clip = lax.axis_size("feat"), lax.axis_size("clip")
    feat, clip = lax.axis_index("feat"), lax.axis_index("clip")
    places, line, core = n_feat // 2, feat // 2, feat % 2
    columns = embeds.shape[1]
    slab, features = frequencies.shape
    outputs = labels.shape[1]
    block = outputs // n_feat
    per_clip = places // n_clip
    scale = math.sqrt(2.0 / (features * n_feat))

    embed_code = encode(embeds.T, EMBED_BOUND)
    weight_rows = weights.T.reshape(per_clip, 2, block, features)
    freq_code = jnp.concatenate(
        [
            part
            for h in range(2)
            for part in (
                encode(frequencies[h * (slab // 2) : (h + 1) * (slab // 2)], FREQ_BOUND),
                encode(weight_rows[:, h].reshape(-1, features), WEIGHT_BOUND),
            )
        ]
    )
    column = (phases * (0.5 / math.pi))[:, None]

    def prepare(codes):
        rows = (slab + weights.shape[1]) // 2
        stacked = jnp.concatenate(
            [code[start + slab // 2 : start + rows] for code in codes for start in range(0, code.shape[0], rows)]
        ).reshape(n_clip, 2, per_clip, block, features)

        def ordered(side):
            rows = lax.dynamic_index_in_dim(stacked, side, 1, keepdims=False).reshape(-1, block, features)
            found = []
            for k in range(places):
                place = line ^ ((places - k) % places)
                at = ((place // per_clip) ^ clip) * per_clip + place % per_clip
                found.append(lax.dynamic_index_in_dim(rows, at, 0, keepdims=False))
            return jnp.concatenate(found)

        def decode(code):
            return code.astype(jnp.float32) * (WEIGHT_BOUND / CODE_MAX)

        own, sent = lax.optimization_barrier((ordered(core), ordered(1 - core)))
        cast = lax.optimization_barrier(decode(jnp.concatenate([own, sent])).astype(jnp.bfloat16))
        return (decode(own), decode(core_swap(sent))), cast

    def share_of(parts):
        parts = parts.reshape(places, block, -1)
        half = parts.astype(jnp.bfloat16)
        total = parts[0]
        found = [line_swap(half[k], places - k) for k in range(1, places)]
        return total, found

    def add_up(total, found):
        for x in found:
            total = total + x.astype(jnp.float32)
        return total

    def gradient_of(residual, phi):
        return lax.dot_general(residual, phi, (((1,), (1,)), ((), ())), preferred_element_type=jnp.float32)

    by_kernels = places == 4 and n_clip == 4 and columns % 16 == 0 and slab == 2 * columns
    phi_of = phi_by_kernels if by_kernels else phi_by_ring
    phi, keep, send, (beta_own, beta_other) = phi_of(
        embed_code, freq_code, column, scale, line, core, clip, prepare
    )
    targets = lax.dynamic_slice_in_dim(labels.T, feat * block, block, 0).astype(jnp.float32)
    there = core_swap(send)
    parts = keep + there.astype(jnp.float32)
    phi_other = core_swap(lax.optimization_barrier((phi, there))[0])
    phi_both = lax.optimization_barrier(jnp.concatenate([phi, phi_other]))
    beta = jnp.concatenate([beta_own, beta_other], axis=1)
    moved = 0.0
    for step in range(STEPS):
        share = (jax.nn.sigmoid(add_up(*share_of(parts))) - targets).astype(jnp.bfloat16)
        residual = jnp.concatenate([share] + [line_swap(share, places - k) for k in range(1, places)])
        grad = gradient_of(residual, phi_both)
        sent = grad.astype(jnp.bfloat16)
        for k in farthest_first(n_clip):
            grad = grad + clip_swap(sent, k).astype(jnp.float32)
        moved = moved + 0.25 * grad
        cast = lax.optimization_barrier((beta - moved).astype(jnp.bfloat16))
        parts = mix(cast, phi_both)
    total, found = share_of(parts)
    ours = moved[:, :features].reshape(places, block, features)
    theirs = core_swap(moved[:, features:]).reshape(places, block, features)
    rows = []
    for b in range(per_clip):
        k = (places - (line ^ (clip * per_clip + b))) % places
        mine = lax.dynamic_index_in_dim(ours, k, 0, keepdims=False)
        their = lax.dynamic_index_in_dim(theirs, k, 0, keepdims=False)
        rows += [jnp.where(core == 0, mine, their), jnp.where(core == 0, their, mine)]
    trained, total = lax.optimization_barrier((weights - jnp.concatenate(rows).T, total))
    return (trained, add_up(total, found).T)


def solution(mesh):
    placed = (P("clip", "feat"), P("clip", "feat"), P("feat"), P("feat", "clip"), P("clip", None))
    return jax.shard_map(
        per_device,
        mesh=mesh,
        in_specs=placed,
        out_specs=(P("feat", "clip"), P("clip", "feat")),
        check_vma=False,
    )
```

```python
import functools
import math

import jax
import jax.numpy as jnp
from jax import lax
from jax.experimental import pallas as pl
from jax.experimental.pallas import tpu as pltpu
from jax.sharding import PartitionSpec as P

STEPS = 2
EMBED_BOUND = 6.0
FREQ_BOUND = 0.5
CODE_MAX = 32766.0
LANES = 128
VMEM_BYTES = 16 * 1024 * 1024
EARLY_VMEM_BYTES = 36 * 1024 * 1024
WEIGHT_BOUND = 6.0
COS_TURNS = (
    0.9999999890590243,
    -19.739204499454,
    64.93911745989858,
    -85.45013953092679,
    60.16763095123224,
    -25.967599249288032,
    6.528658162158786,
)
PER_TURN = EMBED_BOUND * FREQ_BOUND / (CODE_MAX * CODE_MAX * 2.0 * math.pi)


def encode(x, bound):
    return jnp.round(x * (CODE_MAX / bound)).astype(jnp.int16)


def split(code):
    wide = code.astype(jnp.float32)
    high = jnp.round(wide * (1.0 / 256.0)) * 256.0
    return high.astype(jnp.bfloat16), (wide - high).astype(jnp.bfloat16)


def scaled_cos(turns, scale):
    turns = turns - jnp.round(turns)
    square = turns * turns
    value = COS_TURNS[-1] * scale
    for coefficient in COS_TURNS[-2::-1]:
        value = value * square + coefficient * scale
    return value.astype(jnp.bfloat16)


def mix(a, b):
    return jnp.dot(a, b, preferred_element_type=jnp.float32)


def core_swap(x):
    n = lax.axis_size("feat")
    return lax.ppermute(x, "feat", [(i, i ^ 1) for i in range(n)])


def line_swap(x, k):
    n = lax.axis_size("feat")
    return lax.ppermute(x, "feat", [(i, i ^ (2 * k)) for i in range(n)])


def line_move(x, pairs):
    return lax.ppermute(x, "feat", [(2 * a + c, 2 * b + c) for a, b in pairs for c in range(2)])


def clip_swap(x, k):
    n = lax.axis_size("clip")
    return lax.ppermute(x, "clip", [(i, i ^ k) for i in range(n)])


def farthest_first(n):
    return range(n - 1, 0, -1)


def halves(x):
    high = jnp.round(x * (1.0 / 256.0)) * 256.0
    return high.astype(jnp.bfloat16), (x - high).astype(jnp.bfloat16)


def early_kernel(at_ref, *refs, n_embeds, n_freqs, columns):
    embeds, freqs = refs[:n_embeds], refs[n_embeds : n_embeds + n_freqs]
    sum_ref, last_ref, freq_code, f_all, e_all = refs[n_embeds + n_freqs :]
    used = n_embeds * columns
    depth = e_all.shape[0] // 3

    @pl.when(pl.program_id(0) == 0)
    def _():
        line, clip, core = at_ref[0], at_ref[1], at_ref[2]

        def on_ring(place):
            return jnp.where(place == 0, 0, jnp.where(place == 1, 3, place - 1))

        rows = freqs[-1].shape[0]
        pieces = [(ref, h * rows) for ref in freqs[:-2] for h in range(2)] + [(ref, 0) for ref in freqs[-2:]]
        for m in range(len(pieces) // 2):
            step = (on_ring(line) - on_ring(clip ^ m)) & 3
            base = step * 2 * columns + jnp.where(step == 3, depth - used, 0)
            for (ref, start), side in zip(pieces[2 * m : 2 * m + 2], (core, 1 - core)):
                row = pl.multiple_of(base + side * columns, 16)
                freq_code[pl.ds(row, columns), :] = ref[start : start + columns, :]
        if depth > used:
            freq_code[used:depth, :] = jnp.zeros((depth - used, freq_code.shape[1]), jnp.int16)
            for start in range(0, 3 * depth, depth):
                e_all[start + used : start + depth, :] = jnp.zeros((depth - used, e_all.shape[1]), jnp.bfloat16)
        for start in range(0, depth, LANES):
            high, low = halves(freq_code[start : start + LANES, :].T.astype(jnp.float32))
            f_all[:, start : start + LANES] = high
            f_all[:, depth + start : depth + start + LANES] = high
            f_all[:, 2 * depth + start : 2 * depth + start + LANES] = low
        last_ref[...] = freq_code[depth:, :].T

    for i, ref in enumerate(embeds):
        high, low = halves(ref[...].astype(jnp.float32))
        for start, value in ((0, high), (depth, low), (2 * depth, high)):
            e_all[start + i * columns : start + (i + 1) * columns, :] = value
    sum_ref[...] = mix(f_all[...], e_all[...])


def late_kernel(
    sum_ref, own_ref, other_ref, last_ref, phase_ref, beta_ref, phi_ref, keep_ref, send_ref, e_all, f_all, *, scale
):
    columns = own_ref.shape[0]
    depth = 2 * columns
    for i, ref in enumerate((own_ref, other_ref)):
        high, low = halves(ref[...].astype(jnp.float32))
        for start, value in ((0, high), (depth, low), (2 * depth, high)):
            e_all[start + i * columns : start + (i + 1) * columns, :] = value

    @pl.when(pl.program_id(0) == 0)
    def _():
        high, low = halves(last_ref[...].astype(jnp.float32))
        f_all[:, :depth], f_all[:, depth : 2 * depth], f_all[:, 2 * depth :] = high, high, low

    total = sum_ref[...] + mix(f_all[...], e_all[...])
    phi = scaled_cos(total * PER_TURN + phase_ref[...], scale)
    phi_ref[...] = phi
    logits = mix(beta_ref[...], phi)
    half = keep_ref.shape[0]
    keep_ref[...] = logits[:half]
    send_ref[...] = logits[half:].astype(jnp.bfloat16)


def phi_by_kernels(embed_code, freq_code, column, scale, line, core, clip, prepare):
    slabs = 4
    columns, clips = embed_code.shape
    features = freq_code.shape[1]
    tie = lax.optimization_barrier
    rows = freq_code.shape[0] // 2
    freq_x, freq_y = clip_swap(freq_code, 1), clip_swap(freq_code, 2)
    ring = [(0, 2), (2, 3), (3, 1), (1, 0)]
    own = [embed_code]
    for _ in range(slabs - 1):
        own.append(line_move(own[-1], ring))
    other = [core_swap(own[0]), core_swap(own[1])]
    x_again, y_again, other[1] = tie((freq_x, freq_y, other[1]))
    freqs = [freq_code, freq_x, freq_y, clip_swap(x_again[:rows], 2), clip_swap(y_again[rows:], 1)]
    other.append(core_swap(own[2]))
    *freqs, own[2] = tie((*freqs, own[2]))
    betas, cast, targets = prepare(freqs)
    early = [x for pair in zip(own[:3], other) for x in pair]
    used = len(early) * columns
    depth = -(-used // LANES) * LANES
    tile = 512 if clips % 512 == 0 else clips

    def whole(*shape):
        return pl.BlockSpec(shape, lambda i: (0,) * len(shape))

    def by_clips(rows):
        return pl.BlockSpec((rows, tile), lambda i: (0, i))

    summed, freq_last = pl.pallas_call(
        functools.partial(early_kernel, n_embeds=len(early), n_freqs=len(freqs), columns=columns),
        grid=(clips // tile,),
        out_shape=(
            jax.ShapeDtypeStruct((features, clips), jnp.float32),
            jax.ShapeDtypeStruct((features, 2 * columns), jnp.int16),
        ),
        in_specs=[pl.BlockSpec(memory_space=pltpu.SMEM)]
        + [by_clips(columns)] * len(early)
        + [whole(*x.shape) for x in freqs],
        out_specs=(by_clips(features), whole(features, 2 * columns)),
        scratch_shapes=[
            pltpu.VMEM((depth + 2 * columns, features), jnp.int16),
            pltpu.VMEM((features, 3 * depth), jnp.bfloat16),
            pltpu.VMEM((3 * depth, tile), jnp.bfloat16),
        ],
        compiler_params=pltpu.CompilerParams(vmem_limit_bytes=EARLY_VMEM_BYTES),
        cost_estimate=pl.CostEstimate(
            flops=6 * features * depth * clips, bytes_accessed=8 * features * clips, transcendentals=0
        ),
        name="early_angles",
    )(jnp.stack([line, clip, core]).astype(jnp.int32), *early, *freqs)
    last, freq_last = tie((own[3], freq_last))
    cast, betas = tie((cast, betas))
    outputs = cast.shape[0]
    phi, keep, send = pl.pallas_call(
        functools.partial(late_kernel, scale=scale),
        grid=(clips // tile,),
        out_shape=(
            jax.ShapeDtypeStruct((features, clips), jnp.bfloat16),
            jax.ShapeDtypeStruct((outputs // 2, clips), jnp.float32),
            jax.ShapeDtypeStruct((outputs // 2, clips), jnp.bfloat16),
        ),
        in_specs=[
            by_clips(features),
            by_clips(columns),
            by_clips(columns),
            whole(features, 2 * columns),
            whole(features, 1),
            whole(outputs, features),
        ],
        out_specs=(by_clips(features), by_clips(outputs // 2), by_clips(outputs // 2)),
        scratch_shapes=[
            pltpu.VMEM((6 * columns, tile), jnp.bfloat16),
            pltpu.VMEM((features, 6 * columns), jnp.bfloat16),
        ],
        compiler_params=pltpu.CompilerParams(vmem_limit_bytes=VMEM_BYTES),
        cost_estimate=pl.CostEstimate(
            flops=6 * features * 2 * columns * clips, bytes_accessed=6 * features * clips, transcendentals=0
        ),
        name="late_angles",
    )(summed, last, core_swap(last), freq_last, column, cast)
    return phi, keep, send, betas, targets


def phi_by_ring(embed_code, freq_code, column, scale, line, core, clip, prepare):
    places, n_clip = lax.axis_size("feat") // 2, lax.axis_size("clip")
    columns, clips = embed_code.shape
    slab, features = 2 * places * columns // n_clip, freq_code.shape[1]
    freqs = [freq_code] + [clip_swap(freq_code, k) for k in range(1, n_clip)]
    freq_all = jnp.zeros((n_clip * slab, features), jnp.int16)
    for k, piece in enumerate(freqs):
        for h in range(2):
            half = piece[h * (piece.shape[0] // 2) :][: slab // 2]
            freq_all = lax.dynamic_update_slice_in_dim(freq_all, half, (clip ^ k) * slab + h * (slab // 2), 0)
    embed_all = jnp.zeros((2 * places * columns, clips), jnp.int16)
    piece = embed_code
    ring = [(i, (i + 1) % places) for i in range(places)]
    for step in range(places):
        if step:
            piece = line_move(piece, ring)
        base = 2 * ((line - step) % places)
        embed_all = lax.dynamic_update_slice_in_dim(embed_all, piece, (base + core) * columns, 0)
        embed_all = lax.dynamic_update_slice_in_dim(
            embed_all, core_swap(piece), (base + 1 - core) * columns, 0
        )

    def dot0(a, b):
        return lax.dot_general(a, b, (((0,), (0,)), ((), ())), preferred_element_type=jnp.float32)

    embed_high, embed_low = split(embed_all)
    freq_high, freq_low = split(freq_all)
    total = dot0(freq_high, embed_high) + (dot0(freq_high, embed_low) + dot0(freq_low, embed_high))
    phi = scaled_cos(total * PER_TURN + column, scale)
    betas, cast, targets = prepare(freqs)
    logits = mix(cast, phi)
    half = logits.shape[0] // 2
    return phi, logits[:half], logits[half:].astype(jnp.bfloat16), betas, targets


def per_device(embeds, frequencies, phases, weights, labels):
    n_feat, n_clip = lax.axis_size("feat"), lax.axis_size("clip")
    feat, clip = lax.axis_index("feat"), lax.axis_index("clip")
    places, line, core = n_feat // 2, feat // 2, feat % 2
    columns = embeds.shape[1]
    slab, features = frequencies.shape
    outputs = labels.shape[1]
    block = outputs // n_feat
    per_clip = places // n_clip
    scale = math.sqrt(2.0 / (features * n_feat))

    embed_code = encode(embeds.T, EMBED_BOUND)
    weight_rows = weights.T.reshape(per_clip, 2, block, features)
    freq_code = jnp.concatenate(
        [
            part
            for h in range(2)
            for part in (
                encode(frequencies[h * (slab // 2) : (h + 1) * (slab // 2)], FREQ_BOUND),
                encode(weight_rows[:, h].reshape(-1, features), WEIGHT_BOUND),
            )
        ]
    )
    column = (phases * (0.5 / math.pi))[:, None]

    def prepare(codes):
        rows = (slab + weights.shape[1]) // 2
        stacked = jnp.concatenate(
            [code[start + slab // 2 : start + rows] for code in codes for start in range(0, code.shape[0], rows)]
        ).reshape(n_clip, 2, per_clip, block, features)

        def ordered(side):
            rows = lax.dynamic_index_in_dim(stacked, side, 1, keepdims=False).reshape(-1, block, features)
            found = []
            for k in range(places):
                place = line ^ ((places - k) % places)
                at = ((place // per_clip) ^ clip) * per_clip + place % per_clip
                found.append(lax.dynamic_index_in_dim(rows, at, 0, keepdims=False))
            return jnp.concatenate(found)

        def decode(code):
            return code.astype(jnp.float32) * (WEIGHT_BOUND / CODE_MAX)

        own, sent = lax.optimization_barrier((ordered(core), ordered(1 - core)))
        cast = lax.optimization_barrier(decode(jnp.concatenate([own, sent])).astype(jnp.bfloat16))
        targets = lax.dynamic_slice_in_dim(labels.T, feat * block, block, 0).astype(jnp.float32)
        return (decode(own), decode(core_swap(sent))), cast, targets

    def share_of(parts):
        parts = parts.reshape(places, block, -1)
        half = parts.astype(jnp.bfloat16)
        total = parts[0]
        found = [line_swap(half[k], places - k) for k in range(1, places)]
        return total, found

    def add_up(total, found):
        for x in found:
            total = total + x.astype(jnp.float32)
        return total

    def gradient_of(residual, phi):
        return lax.dot_general(residual, phi, (((1,), (1,)), ((), ())), preferred_element_type=jnp.float32)

    by_kernels = places == 4 and n_clip == 4 and columns % 16 == 0 and slab == 2 * columns
    phi_of = phi_by_kernels if by_kernels else phi_by_ring
    phi, keep, send, (beta_own, beta_other), targets = phi_of(
        embed_code, freq_code, column, scale, line, core, clip, prepare
    )
    there = core_swap(send)
    parts = keep + there.astype(jnp.float32)
    phi_other = core_swap(lax.optimization_barrier((phi, there))[0])
    phi_both = lax.optimization_barrier(jnp.concatenate([phi, phi_other]))
    beta = jnp.concatenate([beta_own, beta_other], axis=1)
    moved = 0.0
    for step in range(STEPS):
        share = (jax.nn.sigmoid(add_up(*share_of(parts))) - targets).astype(jnp.bfloat16)
        residual = jnp.concatenate([share] + [line_swap(share, places - k) for k in range(1, places)])
        grad = gradient_of(residual, phi_both)
        sent = grad.astype(jnp.bfloat16)
        for k in farthest_first(n_clip):
            grad = grad + clip_swap(sent, k).astype(jnp.float32)
        moved = moved + 0.25 * grad
        cast = lax.optimization_barrier((beta - moved).astype(jnp.bfloat16))
        parts = mix(cast, phi_both)
    total, found = share_of(parts)
    ours = moved[:, :features].reshape(places, block, features)
    theirs = core_swap(moved[:, features:]).reshape(places, block, features)
    rows = []
    for b in range(per_clip):
        k = (places - (line ^ (clip * per_clip + b))) % places
        mine = lax.dynamic_index_in_dim(ours, k, 0, keepdims=False)
        their = lax.dynamic_index_in_dim(theirs, k, 0, keepdims=False)
        rows += [jnp.where(core == 0, mine, their), jnp.where(core == 0, their, mine)]
    trained, total = lax.optimization_barrier((weights - jnp.concatenate(rows).T, total))
    return (trained, add_up(total, found).T)


def solution(mesh):
    placed = (P("clip", "feat"), P("clip", "feat"), P("feat"), P("feat", "clip"), P("clip", None))
    return jax.shard_map(
        per_device,
        mesh=mesh,
        in_specs=placed,
        out_specs=(P("feat", "clip"), P("clip", "feat")),
        check_vma=False,
    )
```

```python
import functools
import math

import jax
import jax.numpy as jnp
from jax import lax
from jax.experimental import pallas as pl
from jax.experimental.pallas import tpu as pltpu
from jax.sharding import PartitionSpec as P

STEPS = 2
EMBED_BOUND = 6.0
FREQ_BOUND = 0.5
CODE_MAX = 32766.0
LANES = 128
VMEM_BYTES = 16 * 1024 * 1024
EARLY_VMEM_BYTES = 36 * 1024 * 1024
WEIGHT_BOUND = 6.0
COS_TURNS = (
    0.9999999890590243,
    -19.739204499454,
    64.93911745989858,
    -85.45013953092679,
    60.16763095123224,
    -25.967599249288032,
    6.528658162158786,
)
PER_TURN = EMBED_BOUND * FREQ_BOUND / (CODE_MAX * CODE_MAX * 2.0 * math.pi)


def encode(x, bound):
    return jnp.round(x * (CODE_MAX / bound)).astype(jnp.int16)


def split(code):
    wide = code.astype(jnp.float32)
    high = jnp.round(wide * (1.0 / 256.0)) * 256.0
    return high.astype(jnp.bfloat16), (wide - high).astype(jnp.bfloat16)


def scaled_cos(turns, scale):
    turns = turns - jnp.round(turns)
    square = turns * turns
    value = COS_TURNS[-1] * scale
    for coefficient in COS_TURNS[-2::-1]:
        value = value * square + coefficient * scale
    return value.astype(jnp.bfloat16)


def mix(a, b):
    return jnp.dot(a, b, preferred_element_type=jnp.float32)


def core_swap(x):
    n = lax.axis_size("feat")
    return lax.ppermute(x, "feat", [(i, i ^ 1) for i in range(n)])


def line_swap(x, k):
    n = lax.axis_size("feat")
    return lax.ppermute(x, "feat", [(i, i ^ (2 * k)) for i in range(n)])


def line_move(x, pairs):
    return lax.ppermute(x, "feat", [(2 * a + c, 2 * b + c) for a, b in pairs for c in range(2)])


def clip_swap(x, k):
    n = lax.axis_size("clip")
    return lax.ppermute(x, "clip", [(i, i ^ k) for i in range(n)])


def farthest_first(n):
    return range(n - 1, 0, -1)


def halves(x):
    high = jnp.round(x * (1.0 / 256.0)) * 256.0
    return high.astype(jnp.bfloat16), (x - high).astype(jnp.bfloat16)


def early_kernel(at_ref, *refs, n_embeds, n_freqs, columns):
    embeds, freqs = refs[:n_embeds], refs[n_embeds : n_embeds + n_freqs]
    sum_ref, last_ref, freq_code, f_all, e_all = refs[n_embeds + n_freqs :]
    used = n_embeds * columns
    depth = e_all.shape[0] // 3

    @pl.when(pl.program_id(0) == 0)
    def _():
        line, clip, core = at_ref[0], at_ref[1], at_ref[2]

        def on_ring(place):
            return jnp.where(place == 0, 0, jnp.where(place == 1, 3, place - 1))

        rows = freqs[-1].shape[0]
        pieces = [(ref, h * rows) for ref in freqs[:-2] for h in range(2)] + [(ref, 0) for ref in freqs[-2:]]
        for m in range(len(pieces) // 2):
            step = (on_ring(line) - on_ring(clip ^ m)) & 3
            base = step * 2 * columns + jnp.where(step == 3, depth - used, 0)
            for (ref, start), side in zip(pieces[2 * m : 2 * m + 2], (core, 1 - core)):
                row = pl.multiple_of(base + side * columns, 16)
                freq_code[pl.ds(row, columns), :] = ref[start : start + columns, :]
        if depth > used:
            freq_code[used:depth, :] = jnp.zeros((depth - used, freq_code.shape[1]), jnp.int16)
            for start in range(0, 3 * depth, depth):
                e_all[start + used : start + depth, :] = jnp.zeros((depth - used, e_all.shape[1]), jnp.bfloat16)
        for start in range(0, depth, LANES):
            high, low = halves(freq_code[start : start + LANES, :].T.astype(jnp.float32))
            f_all[:, start : start + LANES] = high
            f_all[:, depth + start : depth + start + LANES] = high
            f_all[:, 2 * depth + start : 2 * depth + start + LANES] = low
        last_ref[...] = freq_code[depth:, :].T

    for i, ref in enumerate(embeds):
        high, low = halves(ref[...].astype(jnp.float32))
        for start, value in ((0, high), (depth, low), (2 * depth, high)):
            e_all[start + i * columns : start + (i + 1) * columns, :] = value
    sum_ref[...] = mix(f_all[...], e_all[...])


def late_kernel(
    sum_ref, own_ref, other_ref, last_ref, phase_ref, beta_ref, phi_ref, keep_ref, send_ref, e_all, f_all, *, scale
):
    columns = own_ref.shape[0]
    depth = 2 * columns
    for i, ref in enumerate((own_ref, other_ref)):
        high, low = halves(ref[...].astype(jnp.float32))
        for start, value in ((0, high), (depth, low), (2 * depth, high)):
            e_all[start + i * columns : start + (i + 1) * columns, :] = value

    @pl.when(pl.program_id(0) == 0)
    def _():
        high, low = halves(last_ref[...].astype(jnp.float32))
        f_all[:, :depth], f_all[:, depth : 2 * depth], f_all[:, 2 * depth :] = high, high, low

    total = sum_ref[...] + mix(f_all[...], e_all[...])
    phi = scaled_cos(total * PER_TURN + phase_ref[...], scale)
    phi_ref[...] = phi
    logits = mix(beta_ref[...], phi)
    half = keep_ref.shape[0]
    keep_ref[...] = logits[:half]
    send_ref[...] = logits[half:].astype(jnp.bfloat16)


def phi_by_kernels(embed_code, freq_code, column, scale, line, core, clip, prepare):
    slabs = 4
    columns, clips = embed_code.shape
    features = freq_code.shape[1]
    tie = lax.optimization_barrier
    rows = freq_code.shape[0] // 2
    freq_x, freq_y = clip_swap(freq_code, 1), clip_swap(freq_code, 2)
    ring = [(0, 2), (2, 3), (3, 1), (1, 0)]
    own = [embed_code]
    for _ in range(slabs - 1):
        own.append(line_move(own[-1], ring))
    other = [core_swap(own[0]), core_swap(own[1])]
    x_again, other[1] = tie((freq_x, other[1]))
    half_x = clip_swap(x_again[:rows], 2)
    y_again, half_x_first = tie((freq_y, x_again[:rows]))
    freqs = [freq_code, freq_x, freq_y, half_x, clip_swap(y_again[rows:], 1)]
    other.append(core_swap(own[2]))
    *freqs, own[2] = tie((*freqs, own[2]))
    betas, cast, targets = prepare(freqs)
    early = [x for pair in zip(own[:3], other) for x in pair]
    used = len(early) * columns
    depth = -(-used // LANES) * LANES
    tile = clips

    def whole(*shape):
        return pl.BlockSpec(shape, lambda i: (0,) * len(shape))

    def by_clips(rows):
        return pl.BlockSpec((rows, tile), lambda i: (0, i))

    summed, freq_last = pl.pallas_call(
        functools.partial(early_kernel, n_embeds=len(early), n_freqs=len(freqs), columns=columns),
        grid=(clips // tile,),
        out_shape=(
            jax.ShapeDtypeStruct((features, clips), jnp.float32),
            jax.ShapeDtypeStruct((features, 2 * columns), jnp.int16),
        ),
        in_specs=[pl.BlockSpec(memory_space=pltpu.SMEM)]
        + [by_clips(columns)] * len(early)
        + [whole(*x.shape) for x in freqs],
        out_specs=(by_clips(features), whole(features, 2 * columns)),
        scratch_shapes=[
            pltpu.VMEM((depth + 2 * columns, features), jnp.int16),
            pltpu.VMEM((features, 3 * depth), jnp.bfloat16),
            pltpu.VMEM((3 * depth, tile), jnp.bfloat16),
        ],
        compiler_params=pltpu.CompilerParams(vmem_limit_bytes=EARLY_VMEM_BYTES),
        cost_estimate=pl.CostEstimate(
            flops=6 * features * depth * clips, bytes_accessed=8 * features * clips, transcendentals=0
        ),
        name="early_angles",
    )(jnp.stack([line, clip, core]).astype(jnp.int32), *early, *freqs)
    last, freq_last = tie((own[3], freq_last))
    cast, betas = tie((cast, betas))
    outputs = cast.shape[0]
    phi, keep, send = pl.pallas_call(
        functools.partial(late_kernel, scale=scale),
        grid=(clips // tile,),
        out_shape=(
            jax.ShapeDtypeStruct((features, clips), jnp.bfloat16),
            jax.ShapeDtypeStruct((outputs // 2, clips), jnp.float32),
            jax.ShapeDtypeStruct((outputs // 2, clips), jnp.bfloat16),
        ),
        in_specs=[
            by_clips(features),
            by_clips(columns),
            by_clips(columns),
            whole(features, 2 * columns),
            whole(features, 1),
            whole(outputs, features),
        ],
        out_specs=(by_clips(features), by_clips(outputs // 2), by_clips(outputs // 2)),
        scratch_shapes=[
            pltpu.VMEM((6 * columns, tile), jnp.bfloat16),
            pltpu.VMEM((features, 6 * columns), jnp.bfloat16),
        ],
        compiler_params=pltpu.CompilerParams(vmem_limit_bytes=VMEM_BYTES),
        cost_estimate=pl.CostEstimate(
            flops=6 * features * 2 * columns * clips, bytes_accessed=6 * features * clips, transcendentals=0
        ),
        name="late_angles",
    )(summed, last, core_swap(last), freq_last, column, cast)
    return phi, keep, send, betas, targets


def phi_by_ring(embed_code, freq_code, column, scale, line, core, clip, prepare):
    places, n_clip = lax.axis_size("feat") // 2, lax.axis_size("clip")
    columns, clips = embed_code.shape
    slab, features = 2 * places * columns // n_clip, freq_code.shape[1]
    freqs = [freq_code] + [clip_swap(freq_code, k) for k in range(1, n_clip)]
    freq_all = jnp.zeros((n_clip * slab, features), jnp.int16)
    for k, piece in enumerate(freqs):
        for h in range(2):
            half = piece[h * (piece.shape[0] // 2) :][: slab // 2]
            freq_all = lax.dynamic_update_slice_in_dim(freq_all, half, (clip ^ k) * slab + h * (slab // 2), 0)
    embed_all = jnp.zeros((2 * places * columns, clips), jnp.int16)
    piece = embed_code
    ring = [(i, (i + 1) % places) for i in range(places)]
    for step in range(places):
        if step:
            piece = line_move(piece, ring)
        base = 2 * ((line - step) % places)
        embed_all = lax.dynamic_update_slice_in_dim(embed_all, piece, (base + core) * columns, 0)
        embed_all = lax.dynamic_update_slice_in_dim(
            embed_all, core_swap(piece), (base + 1 - core) * columns, 0
        )

    def dot0(a, b):
        return lax.dot_general(a, b, (((0,), (0,)), ((), ())), preferred_element_type=jnp.float32)

    embed_high, embed_low = split(embed_all)
    freq_high, freq_low = split(freq_all)
    total = dot0(freq_high, embed_high) + (dot0(freq_high, embed_low) + dot0(freq_low, embed_high))
    phi = scaled_cos(total * PER_TURN + column, scale)
    betas, cast, targets = prepare(freqs)
    logits = mix(cast, phi)
    half = logits.shape[0] // 2
    return phi, logits[:half], logits[half:].astype(jnp.bfloat16), betas, targets


def per_device(embeds, frequencies, phases, weights, labels):
    n_feat, n_clip = lax.axis_size("feat"), lax.axis_size("clip")
    feat, clip = lax.axis_index("feat"), lax.axis_index("clip")
    places, line, core = n_feat // 2, feat // 2, feat % 2
    columns = embeds.shape[1]
    slab, features = frequencies.shape
    outputs = labels.shape[1]
    block = outputs // n_feat
    per_clip = places // n_clip
    scale = math.sqrt(2.0 / (features * n_feat))

    embed_code = encode(embeds.T, EMBED_BOUND)
    weight_rows = weights.T.reshape(per_clip, 2, block, features)
    freq_code = jnp.concatenate(
        [
            part
            for h in range(2)
            for part in (
                encode(frequencies[h * (slab // 2) : (h + 1) * (slab // 2)], FREQ_BOUND),
                encode(weight_rows[:, h].reshape(-1, features), WEIGHT_BOUND),
            )
        ]
    )
    column = (phases * (0.5 / math.pi))[:, None]

    def prepare(codes):
        rows = (slab + weights.shape[1]) // 2
        stacked = jnp.concatenate(
            [code[start + slab // 2 : start + rows] for code in codes for start in range(0, code.shape[0], rows)]
        ).reshape(n_clip, 2, per_clip, block, features)

        def ordered(side):
            rows = lax.dynamic_index_in_dim(stacked, side, 1, keepdims=False).reshape(-1, block, features)
            found = []
            for k in range(places):
                place = line ^ ((places - k) % places)
                at = ((place // per_clip) ^ clip) * per_clip + place % per_clip
                found.append(lax.dynamic_index_in_dim(rows, at, 0, keepdims=False))
            return jnp.concatenate(found)

        def decode(code):
            return code.astype(jnp.float32) * (WEIGHT_BOUND / CODE_MAX)

        own, sent = lax.optimization_barrier((ordered(core), ordered(1 - core)))
        cast = lax.optimization_barrier(decode(jnp.concatenate([own, sent])).astype(jnp.bfloat16))
        targets = lax.dynamic_slice_in_dim(labels.T, feat * block, block, 0).astype(jnp.float32)
        return (decode(own), decode(core_swap(sent))), cast, targets

    def share_of(parts):
        parts = parts.reshape(places, block, -1)
        half = parts.astype(jnp.bfloat16)
        total = parts[0]
        found = [line_swap(half[k], places - k) for k in range(1, places)]
        return total, found

    def add_up(total, found):
        for x in found:
            total = total + x.astype(jnp.float32)
        return total

    def gradient_of(residual, phi):
        return lax.dot_general(residual, phi, (((1,), (1,)), ((), ())), preferred_element_type=jnp.float32)

    by_kernels = places == 4 and n_clip == 4 and columns % 16 == 0 and slab == 2 * columns
    phi_of = phi_by_kernels if by_kernels else phi_by_ring
    phi, keep, send, (beta_own, beta_other), targets = phi_of(
        embed_code, freq_code, column, scale, line, core, clip, prepare
    )
    there = core_swap(send)
    parts = keep + there.astype(jnp.float32)
    phi_other = core_swap(lax.optimization_barrier((phi, there))[0])
    phi_both = lax.optimization_barrier(jnp.concatenate([phi, phi_other]))
    beta = jnp.concatenate([beta_own, beta_other], axis=1)
    moved = 0.0
    for step in range(STEPS):
        share = (jax.nn.sigmoid(add_up(*share_of(parts))) - targets).astype(jnp.bfloat16)
        residual = jnp.concatenate([share] + [line_swap(share, places - k) for k in range(1, places)])
        grad = gradient_of(residual, phi_both)
        sent = grad.astype(jnp.bfloat16)
        for k in farthest_first(n_clip):
            grad = grad + clip_swap(sent, k).astype(jnp.float32)
        moved = moved + 0.25 * grad
        cast = lax.optimization_barrier((beta - moved).astype(jnp.bfloat16))
        parts = mix(cast, phi_both)
    total, found = share_of(parts)
    ours = moved[:, :features].reshape(places, block, features)
    theirs = core_swap(moved[:, features:]).reshape(places, block, features)
    rows = []
    for b in range(per_clip):
        k = (places - (line ^ (clip * per_clip + b))) % places
        mine = lax.dynamic_index_in_dim(ours, k, 0, keepdims=False)
        their = lax.dynamic_index_in_dim(theirs, k, 0, keepdims=False)
        rows += [jnp.where(core == 0, mine, their), jnp.where(core == 0, their, mine)]
    trained, total = lax.optimization_barrier((weights - jnp.concatenate(rows).T, total))
    return (trained, add_up(total, found).T)


def solution(mesh):
    placed = (P("clip", "feat"), P("clip", "feat"), P("feat"), P("feat", "clip"), P("clip", None))
    return jax.shard_map(
        per_device,
        mesh=mesh,
        in_specs=placed,
        out_specs=(P("feat", "clip"), P("clip", "feat")),
        check_vma=False,
    )
```

```python
import functools
import math

import jax
import jax.numpy as jnp
from jax import lax
from jax.experimental import pallas as pl
from jax.experimental.pallas import tpu as pltpu
from jax.sharding import PartitionSpec as P

STEPS = 2
EMBED_BOUND = 6.0
FREQ_BOUND = 0.5
CODE_MAX = 32766.0
LANES = 128
VMEM_BYTES = 16 * 1024 * 1024
EARLY_VMEM_BYTES = 28 * 1024 * 1024
WEIGHT_BOUND = 6.0
COS_TURNS = (
    0.9999992107823231,
    -19.738980355764067,
    64.9286574210343,
    -85.27162153430471,
    58.790492120138815,
    -21.07110562713763,
)
PER_TURN = EMBED_BOUND * FREQ_BOUND / (CODE_MAX * CODE_MAX * 2.0 * math.pi)


def encode(x, bound):
    return jnp.round(x * (CODE_MAX / bound)).astype(jnp.int16)


def split(code):
    wide = code.astype(jnp.float32)
    high = jnp.round(wide * (1.0 / 256.0)) * 256.0
    return high.astype(jnp.bfloat16), (wide - high).astype(jnp.bfloat16)


def scaled_cos(turns, scale):
    turns = turns - jnp.round(turns)
    square = turns * turns
    value = COS_TURNS[-1] * scale
    for coefficient in COS_TURNS[-2::-1]:
        value = value * square + coefficient * scale
    return value.astype(jnp.bfloat16)


def mix(a, b):
    return jnp.dot(a, b, preferred_element_type=jnp.float32)


def core_swap(x):
    n = lax.axis_size("feat")
    return lax.ppermute(x, "feat", [(i, i ^ 1) for i in range(n)])


def line_swap(x, k):
    n = lax.axis_size("feat")
    return lax.ppermute(x, "feat", [(i, i ^ (2 * k)) for i in range(n)])


def line_move(x, pairs):
    return lax.ppermute(x, "feat", [(2 * a + c, 2 * b + c) for a, b in pairs for c in range(2)])


def clip_swap(x, k):
    n = lax.axis_size("clip")
    return lax.ppermute(x, "clip", [(i, i ^ k) for i in range(n)])


def farthest_first(n):
    return range(n - 1, 0, -1)


def halves(x):
    high = jnp.round(x * (1.0 / 256.0)) * 256.0
    return high.astype(jnp.bfloat16), (x - high).astype(jnp.bfloat16)


def early_kernel(at_ref, *refs, n_embeds, n_freqs, columns):
    embeds, freqs = refs[:n_embeds], refs[n_embeds : n_embeds + n_freqs]
    sum_ref, last_ref, freq_code, f_all, e_all = refs[n_embeds + n_freqs :]
    used = n_embeds * columns
    depth = e_all.shape[0] // 3

    @pl.when(pl.program_id(0) == 0)
    def _():
        line, clip, core = at_ref[0], at_ref[1], at_ref[2]

        def on_ring(place):
            return jnp.where(place == 0, 0, jnp.where(place == 1, 3, place - 1))

        rows = freqs[-1].shape[0]
        pieces = [(ref, h * rows) for ref in freqs[:-2] for h in range(2)] + [(ref, 0) for ref in freqs[-2:]]
        for m in range(len(pieces) // 2):
            step = (on_ring(line) - on_ring(clip ^ m)) & 3
            base = step * 2 * columns + jnp.where(step == 3, depth - used, 0)
            for (ref, start), side in zip(pieces[2 * m : 2 * m + 2], (core, 1 - core)):
                row = pl.multiple_of(base + side * columns, 16)
                freq_code[pl.ds(row, columns), :] = ref[start : start + columns, :]
        if depth > used:
            freq_code[used:depth, :] = jnp.zeros((depth - used, freq_code.shape[1]), jnp.int16)
            for start in range(0, 3 * depth, depth):
                e_all[start + used : start + depth, :] = jnp.zeros((depth - used, e_all.shape[1]), jnp.bfloat16)
        for start in range(0, depth, LANES):
            high, low = halves(freq_code[start : start + LANES, :].T.astype(jnp.float32))
            f_all[:, start : start + LANES] = high
            f_all[:, depth + start : depth + start + LANES] = high
            f_all[:, 2 * depth + start : 2 * depth + start + LANES] = low
        last_ref[...] = freq_code[depth:, :].T

    for i, ref in enumerate(embeds):
        high, low = halves(ref[...].astype(jnp.float32))
        for start, value in ((0, high), (depth, low), (2 * depth, high)):
            e_all[start + i * columns : start + (i + 1) * columns, :] = value
    sum_ref[...] = mix(f_all[...], e_all[...])


def late_kernel(
    sum_ref, own_ref, other_ref, last_ref, phase_ref, beta_ref, phi_ref, keep_ref, send_ref, e_all, f_all, *, scale
):
    columns = own_ref.shape[0]
    depth = 2 * columns
    for i, ref in enumerate((own_ref, other_ref)):
        high, low = halves(ref[...].astype(jnp.float32))
        for start, value in ((0, high), (depth, low), (2 * depth, high)):
            e_all[start + i * columns : start + (i + 1) * columns, :] = value

    @pl.when(pl.program_id(0) == 0)
    def _():
        high, low = halves(last_ref[...].astype(jnp.float32))
        f_all[:, :depth], f_all[:, depth : 2 * depth], f_all[:, 2 * depth :] = high, high, low

    total = sum_ref[...] + mix(f_all[...], e_all[...])
    phi = scaled_cos(total * PER_TURN + phase_ref[...], scale)
    phi_ref[...] = phi
    logits = mix(beta_ref[...], phi)
    half = keep_ref.shape[0]
    keep_ref[...] = logits[:half]
    send_ref[...] = logits[half:].astype(jnp.bfloat16)


def phi_by_kernels(embed_code, freq_code, column, scale, line, core, clip, prepare):
    slabs = 4
    columns, clips = embed_code.shape
    features = freq_code.shape[1]
    tie = lax.optimization_barrier
    rows = freq_code.shape[0] // 2
    freq_x, freq_y = clip_swap(freq_code, 1), clip_swap(freq_code, 2)
    ring = [(0, 2), (2, 3), (3, 1), (1, 0)]
    own = [embed_code]
    for _ in range(slabs - 1):
        own.append(line_move(own[-1], ring))
    other = [core_swap(own[0]), core_swap(own[1])]
    x_again, other[1] = tie((freq_x, other[1]))
    half_x = clip_swap(x_again[:rows], 2)
    y_again, half_x_first = tie((freq_y, x_again[:rows]))
    freqs = [freq_code, freq_x, freq_y, half_x, clip_swap(y_again[rows:], 1)]
    other.append(core_swap(own[2]))
    *freqs, own[2] = tie((*freqs, own[2]))
    betas, cast, targets = prepare(freqs)
    early = [x for pair in zip(own[:3], other) for x in pair]
    used = len(early) * columns
    depth = -(-used // LANES) * LANES
    tile = clips

    def whole(*shape):
        return pl.BlockSpec(shape, lambda i: (0,) * len(shape))

    def by_clips(rows):
        return pl.BlockSpec((rows, tile), lambda i: (0, i))

    summed, freq_last = pl.pallas_call(
        functools.partial(early_kernel, n_embeds=len(early), n_freqs=len(freqs), columns=columns),
        grid=(clips // tile,),
        out_shape=(
            jax.ShapeDtypeStruct((features, clips), jnp.float32),
            jax.ShapeDtypeStruct((features, 2 * columns), jnp.int16),
        ),
        in_specs=[pl.BlockSpec(memory_space=pltpu.SMEM)]
        + [by_clips(columns)] * len(early)
        + [whole(*x.shape) for x in freqs],
        out_specs=(by_clips(features), whole(features, 2 * columns)),
        scratch_shapes=[
            pltpu.VMEM((depth + 2 * columns, features), jnp.int16),
            pltpu.VMEM((features, 3 * depth), jnp.bfloat16),
            pltpu.VMEM((3 * depth, tile), jnp.bfloat16),
        ],
        compiler_params=pltpu.CompilerParams(vmem_limit_bytes=EARLY_VMEM_BYTES),
        cost_estimate=pl.CostEstimate(
            flops=6 * features * depth * clips, bytes_accessed=8 * features * clips, transcendentals=0
        ),
        name="early_angles",
    )(jnp.stack([line, clip, core]).astype(jnp.int32), *early, *freqs)
    last, freq_last = tie((own[3], freq_last))
    cast, betas = tie((cast, betas))
    outputs = cast.shape[0]
    phi, keep, send = pl.pallas_call(
        functools.partial(late_kernel, scale=scale),
        grid=(clips // tile,),
        out_shape=(
            jax.ShapeDtypeStruct((features, clips), jnp.bfloat16),
            jax.ShapeDtypeStruct((outputs // 2, clips), jnp.float32),
            jax.ShapeDtypeStruct((outputs // 2, clips), jnp.bfloat16),
        ),
        in_specs=[
            by_clips(features),
            by_clips(columns),
            by_clips(columns),
            whole(features, 2 * columns),
            whole(features, 1),
            whole(outputs, features),
        ],
        out_specs=(by_clips(features), by_clips(outputs // 2), by_clips(outputs // 2)),
        scratch_shapes=[
            pltpu.VMEM((6 * columns, tile), jnp.bfloat16),
            pltpu.VMEM((features, 6 * columns), jnp.bfloat16),
        ],
        compiler_params=pltpu.CompilerParams(vmem_limit_bytes=VMEM_BYTES),
        cost_estimate=pl.CostEstimate(
            flops=6 * features * 2 * columns * clips, bytes_accessed=6 * features * clips, transcendentals=0
        ),
        name="late_angles",
    )(summed, last, core_swap(last), freq_last, column, cast)
    return phi, keep, send, betas, targets


def phi_by_ring(embed_code, freq_code, column, scale, line, core, clip, prepare):
    places, n_clip = lax.axis_size("feat") // 2, lax.axis_size("clip")
    columns, clips = embed_code.shape
    slab, features = 2 * places * columns // n_clip, freq_code.shape[1]
    freqs = [freq_code] + [clip_swap(freq_code, k) for k in range(1, n_clip)]
    freq_all = jnp.zeros((n_clip * slab, features), jnp.int16)
    for k, piece in enumerate(freqs):
        for h in range(2):
            half = piece[h * (piece.shape[0] // 2) :][: slab // 2]
            freq_all = lax.dynamic_update_slice_in_dim(freq_all, half, (clip ^ k) * slab + h * (slab // 2), 0)
    embed_all = jnp.zeros((2 * places * columns, clips), jnp.int16)
    piece = embed_code
    ring = [(i, (i + 1) % places) for i in range(places)]
    for step in range(places):
        if step:
            piece = line_move(piece, ring)
        base = 2 * ((line - step) % places)
        embed_all = lax.dynamic_update_slice_in_dim(embed_all, piece, (base + core) * columns, 0)
        embed_all = lax.dynamic_update_slice_in_dim(
            embed_all, core_swap(piece), (base + 1 - core) * columns, 0
        )

    def dot0(a, b):
        return lax.dot_general(a, b, (((0,), (0,)), ((), ())), preferred_element_type=jnp.float32)

    embed_high, embed_low = split(embed_all)
    freq_high, freq_low = split(freq_all)
    total = dot0(freq_high, embed_high) + (dot0(freq_high, embed_low) + dot0(freq_low, embed_high))
    phi = scaled_cos(total * PER_TURN + column, scale)
    betas, cast, targets = prepare(freqs)
    logits = mix(cast, phi)
    half = logits.shape[0] // 2
    return phi, logits[:half], logits[half:].astype(jnp.bfloat16), betas, targets


def per_device(embeds, frequencies, phases, weights, labels):
    n_feat, n_clip = lax.axis_size("feat"), lax.axis_size("clip")
    feat, clip = lax.axis_index("feat"), lax.axis_index("clip")
    places, line, core = n_feat // 2, feat // 2, feat % 2
    columns = embeds.shape[1]
    slab, features = frequencies.shape
    outputs = labels.shape[1]
    block = outputs // n_feat
    per_clip = places // n_clip
    scale = math.sqrt(2.0 / (features * n_feat))

    embed_code = encode(embeds.T, EMBED_BOUND)
    weight_rows = weights.T.reshape(per_clip, 2, block, features)
    freq_code = jnp.concatenate(
        [
            part
            for h in range(2)
            for part in (
                encode(frequencies[h * (slab // 2) : (h + 1) * (slab // 2)], FREQ_BOUND),
                encode(weight_rows[:, h].reshape(-1, features), WEIGHT_BOUND),
            )
        ]
    )
    column = (phases * (0.5 / math.pi))[:, None]

    def prepare(codes):
        rows = (slab + weights.shape[1]) // 2
        stacked = jnp.concatenate(
            [code[start + slab // 2 : start + rows] for code in codes for start in range(0, code.shape[0], rows)]
        ).reshape(n_clip, 2, per_clip, block, features)

        def ordered(side):
            rows = lax.dynamic_index_in_dim(stacked, side, 1, keepdims=False).reshape(-1, block, features)
            found = []
            for k in range(places):
                place = line ^ ((places - k) % places)
                at = ((place // per_clip) ^ clip) * per_clip + place % per_clip
                found.append(lax.dynamic_index_in_dim(rows, at, 0, keepdims=False))
            return jnp.concatenate(found)

        def decode(code):
            return code.astype(jnp.float32) * (WEIGHT_BOUND / CODE_MAX)

        own, sent = lax.optimization_barrier((ordered(core), ordered(1 - core)))
        cast = lax.optimization_barrier(decode(jnp.concatenate([own, sent])).astype(jnp.bfloat16))
        targets = lax.dynamic_slice_in_dim(labels.T, feat * block, block, 0).astype(jnp.float32)
        return (decode(own), decode(core_swap(sent))), cast, targets

    def share_of(parts):
        parts = parts.reshape(places, block, -1)
        half = parts.astype(jnp.bfloat16)
        total = parts[0]
        found = [line_swap(half[k], places - k) for k in range(1, places)]
        return total, found

    def add_up(total, found):
        for x in found:
            total = total + x.astype(jnp.float32)
        return total

    def gradient_of(residual, phi):
        return lax.dot_general(residual, phi, (((1,), (1,)), ((), ())), preferred_element_type=jnp.float32)

    by_kernels = places == 4 and n_clip == 4 and columns % 16 == 0 and slab == 2 * columns
    phi_of = phi_by_kernels if by_kernels else phi_by_ring
    phi, keep, send, (beta_own, beta_other), targets = phi_of(
        embed_code, freq_code, column, scale, line, core, clip, prepare
    )
    there = core_swap(send)
    parts = keep + there.astype(jnp.float32)
    phi_other = core_swap(lax.optimization_barrier((phi, there))[0])
    phi_both = lax.optimization_barrier(jnp.concatenate([phi, phi_other]))
    beta = jnp.concatenate([beta_own, beta_other], axis=1)
    moved = 0.0
    for step in range(STEPS):
        share = (jax.nn.sigmoid(add_up(*share_of(parts))) - targets).astype(jnp.bfloat16)
        residual = jnp.concatenate([share] + [line_swap(share, places - k) for k in range(1, places)])
        grad = gradient_of(residual, phi_both)
        sent = grad.astype(jnp.bfloat16)
        for k in farthest_first(n_clip):
            grad = grad + clip_swap(sent, k).astype(jnp.float32)
        moved = moved + 0.25 * grad
        cast = lax.optimization_barrier((beta - moved).astype(jnp.bfloat16))
        parts = mix(cast, phi_both)
    total, found = share_of(parts)
    ours = moved[:, :features].reshape(places, block, features)
    theirs = core_swap(moved[:, features:]).reshape(places, block, features)
    rows = []
    for b in range(per_clip):
        k = (places - (line ^ (clip * per_clip + b))) % places
        mine = lax.dynamic_index_in_dim(ours, k, 0, keepdims=False)
        their = lax.dynamic_index_in_dim(theirs, k, 0, keepdims=False)
        rows += [jnp.where(core == 0, mine, their), jnp.where(core == 0, their, mine)]
    trained, total = lax.optimization_barrier((weights - jnp.concatenate(rows).T, total))
    return (trained, add_up(total, found).T)


def solution(mesh):
    placed = (P("clip", "feat"), P("clip", "feat"), P("feat"), P("feat", "clip"), P("clip", None))
    return jax.shard_map(
        per_device,
        mesh=mesh,
        in_specs=placed,
        out_specs=(P("feat", "clip"), P("clip", "feat")),
        check_vma=False,
    )
```
